32 devices in a mesh: seq: 16 (over z, y, x), head: 2 (over core).
Axes of the slice: x: 2, y: 2, z: 4, core: 2. Of those that a mesh axis runs over, the one named last changes fastest.
Arguments:
- activations: bfloat16 [8192, 2048], P('seq', 'head'), may hold values from -6 to 6
- w_proj: bfloat16 [3, 2048, 2048], P(None, None, 'head'), may hold values from -0.125 to 0.125
- level_weight: float32 [8192, 16, 14], P('seq', 'head'), may hold values from 0.25 to 4
- grad_out: bfloat16 [8192, 2048], P('seq', 'head'), may hold values from -6 to 6
Outputs:
- attn_output: bfloat16 [8192, 2048], P('seq', 'head')
- grad_query: bfloat16 [8192, 2048], P('seq', 'head')
- grad_key: bfloat16 [8192, 2048], P('seq', 'head')
- grad_value: bfloat16 [8192, 2048], P('seq', 'head')
The draws below stay inside these ranges and needn't reach their ends.
All inputs are finite; a program needn't handle non-finite values.
Results may differ from the reference program's by a relative error of at most 0.0085.
Values may be sent and summed in bfloat16 or wider, within the bound.
A program may use at most 64 MiB of HBM per device.

```python
import math
import jax
import jax.numpy as jnp
from jax import lax

D = 2048
HEADS = 16
HEAD_DIM = 128
TOK_DEV = 512
TOKENS = 8192
LEVELS = 14
N_SEQ = 16


def steps_of(stream_key, extent, shards, least, top_value):
    factor_of = 1.0
    for position, shards_of in shards:
        steps = jax.random.uniform(jax.random.fold_in(jax.random.fold_in(stream_key, 6), position), (shards_of,), jnp.float32, least / len(shards), top_value / len(shards))
        factor_of = factor_of * jnp.repeat(jnp.exp(steps), extent[position] // shards_of).reshape((-1,) + (1,) * (len(extent) - 1 - position))
    return factor_of


def bell_draw(key, dims, scale, bound, pieces=(), held_as=jnp.bfloat16):
    loudness = steps_of(key, dims, pieces, -0.22, 0.18) if pieces else 1.0
    values = jax.random.normal(key, dims, jnp.float32) * scale * loudness
    return jnp.minimum(jnp.maximum(values, -bound), bound).astype(held_as)


def setup_inputs(seed: int = 0) -> dict:
    seeds = jax.random.split(jax.random.key(seed), 5)
    activations = bell_draw(seeds[0], (TOKENS, D), 1.0, 6.0, ((0, 16), (1, 2)))
    w_proj = bell_draw(seeds[1], (3, D, D), D ** -0.5, 0.125, ((2, 2),))
    level_weight = jnp.clip(jnp.exp(math.log(4.0) - 2.7725887 * jax.random.uniform(seeds[2], (TOKENS, HEADS, LEVELS), jnp.float32) ** steps_of(seeds[2], (TOKENS, HEADS, LEVELS), ((0, 16), (1, 2)), -0.2, 0.2)), 0.25, 4.0)
    grad_out = bell_draw(seeds[3], (TOKENS, D), 1.0, 6.0, ((0, 16), (1, 2)))
    return dict(activations=activations, w_proj=w_proj, level_weight=level_weight, grad_out=grad_out)


def bit_length_of(numbers, width):
    total = jnp.zeros_like(numbers)
    for shift_by in range(width):
        total = total + (jnp.right_shift(numbers, shift_by) > 0).astype(jnp.int32)
    return total


def level_factors(count):
    index_list = jnp.arange(count, dtype=jnp.int32)
    return jnp.exp2(-0.5 * (jnp.maximum(index_list, 1) - 1).astype(jnp.float32))


def reference(activations, w_proj, level_weight, grad_out):
    scale = HEAD_DIM ** -0.5
    block_len = TOK_DEV
    block_bits = TOK_DEV.bit_length() - 1
    seq_bits = N_SEQ.bit_length() - 1
    blocks = N_SEQ
    highest = lax.Precision.HIGHEST

    def split_heads(matrix):
        return matrix.reshape(blocks, block_len, HEADS, HEAD_DIM).transpose(2, 0, 1, 3)

    query_all = split_heads(jnp.dot(activations, w_proj[0], preferred_element_type=jnp.float32).astype(jnp.bfloat16))
    key_all = split_heads(jnp.dot(activations, w_proj[1], preferred_element_type=jnp.float32).astype(jnp.bfloat16))
    value_all = split_heads(jnp.dot(activations, w_proj[2], preferred_element_type=jnp.float32).astype(jnp.bfloat16))
    cotan_all = split_heads(grad_out)
    weight = level_weight * level_factors(LEVELS)
    weight = weight.reshape(blocks, block_len, HEADS, LEVELS).transpose(2, 0, 1, 3)

    local_pos = jnp.arange(block_len, dtype=jnp.int32)
    local_level = bit_length_of(jnp.bitwise_xor(local_pos[:, None], local_pos[None, :]), block_bits)
    causal = local_pos[None, :] <= local_pos[:, None]
    block_ids = jnp.arange(blocks, dtype=jnp.int32)
    differ = jnp.bitwise_xor(block_ids[:, None], block_ids[None, :])
    earlier = block_ids[None, :] < block_ids[:, None]
    select = jnp.stack([earlier & (jnp.right_shift(differ, bit_index) == 1) for bit_index in range(seq_bits)], 1).astype(jnp.float32)

    def one_head(operands):
        query_rows, key_rows, value_rows, cotangent, head_weight = operands
        query_f = query_rows.astype(jnp.float32)
        key_f = key_rows.astype(jnp.float32)
        value_f = value_rows.astype(jnp.float32)
        cotan_f = cotangent.astype(jnp.float32)
        mask_weight = jnp.zeros((blocks, block_len, block_len), jnp.float32)
        for level_ix in range(block_bits + 1):
            chosen = (local_level == level_ix) & causal
            mask_weight = mask_weight + jnp.where(chosen[None], head_weight[:, :, level_ix][:, :, None], 0.0)
        scores = jnp.einsum("ntd,nsd->nts", query_f, key_f) * scale
        attn = (scores * mask_weight).astype(jnp.bfloat16).astype(jnp.float32)
        out_inner = jnp.einsum("nts,nsd->ntd", attn, value_f)
        back = jnp.einsum("ntd,nsd->nts", cotan_f, value_f)
        grads = (back * mask_weight * scale).astype(jnp.bfloat16).astype(jnp.float32)
        dq_inner = jnp.einsum("nts,nsd->ntd", grads, key_f)
        dk_inner = jnp.einsum("nts,ntd->nsd", grads, query_f)
        dv_inner = jnp.einsum("nts,ntd->nsd", attn, cotan_f)
        cross = head_weight[:, :, block_bits + 1:]
        states = jnp.einsum("nsx,nsy->nxy", key_f, value_f)
        prefix = jnp.einsum("dje,exy->djxy", select, states, precision=highest).astype(jnp.bfloat16).astype(jnp.float32)
        reads = jnp.einsum("ntx,njxy->ntjy", query_f, prefix)
        out_cross = scale * jnp.sum(cross[..., None] * reads, 2)
        reads_back = jnp.einsum("nty,njxy->ntjx", cotan_f, prefix)
        dq_cross = scale * jnp.sum(cross[..., None] * reads_back, 2)
        weighted = cross[:, :, :, None] * query_f[:, :, None, :]
        level_grads = jnp.einsum("ntjx,nty->njxy", weighted, cotan_f, precision=highest)
        suffix = jnp.einsum("dje,djxy->ejxy", select, level_grads, precision=highest).astype(jnp.bfloat16).astype(jnp.float32)
        dk_cross = scale * jnp.einsum("nsy,njxy->nsx", value_f, suffix)
        dv_cross = scale * jnp.einsum("nsx,njxy->nsy", key_f, suffix)
        return (out_inner + out_cross, dq_inner + dq_cross, dk_inner + dk_cross, dv_inner + dv_cross)

    results = lax.map(one_head, (query_all, key_all, value_all, cotan_all, weight))

    def merge_heads(array):
        return array.transpose(1, 2, 0, 3).reshape(TOKENS, D).astype(jnp.bfloat16)

    return (merge_heads(results[0]), merge_heads(results[1]), merge_heads(results[2]), merge_heads(results[3]))
```

```python
import functools

import jax
import jax.numpy as jnp
from jax import lax
from jax.experimental import pallas as pl
from jax.experimental.pallas import tpu as pltpu
from jax.sharding import PartitionSpec as P

MESH = pl.DeviceIdType.MESH
F32 = jnp.float32
BF16 = jnp.bfloat16


def dot_nn(a, b):
    return lax.dot_general(a, b, (((1,), (0,)), ((), ())), preferred_element_type=F32)


def dot_nt(a, b):
    return lax.dot_general(a, b, (((1,), (1,)), ((), ())), preferred_element_type=F32)


def dot_tn(a, b):
    return lax.dot_general(a, b, (((0,), (0,)), ((), ())), preferred_element_type=F32)


def level_factor(level):
    return 2.0 ** (-0.5 * (max(level, 1) - 1))


def diagonal_mask(columns, row, size, leaf, position):
    if size == leaf:
        base, difference = position
        total = jnp.zeros((leaf, leaf), F32)
        for level in range(leaf.bit_length()):
            column = columns[row : row + leaf, level : level + 1]
            total = jnp.where(base == level, column, total)
        return total
    half = size // 2
    upper = diagonal_mask(columns, row, half, leaf, position)
    lower = diagonal_mask(columns, row + half, half, leaf, position)
    level = half.bit_length()
    side = jnp.broadcast_to(columns[row + half : row + size, level : level + 1], (half, half))
    return jnp.concatenate(
        [
            jnp.concatenate([upper, jnp.zeros((half, half), F32)], 1),
            jnp.concatenate([side, lower], 1),
        ],
        0,
    )


def kernel(
    dims,
    act_ref,
    w_ref,
    lw_ref,
    cot_ref,
    out_ref,
    dq_ref,
    dk_ref,
    dv_ref,
    acts,
    w_vm,
    cot,
    wcol,
    qkv,
    wq,
    group,
    rgrad,
    moving,
    s_send,
    s_recv,
    r_send,
    r_recv,
    upper,
    inner,
    act_sem,
    cot_sem,
    w_sem,
    act_send_sem,
    act_recv_sem,
    s_send_sem,
    s_recv_sem,
    r_send_sem,
    r_recv_sem,
):
    n_seq, n_head, heads, head_dim, block, features, per = dims
    chunks = heads // per
    bits = n_seq.bit_length() - 1
    block_bits = block.bit_length() - 1
    scale = head_dim**-0.5
    width = per * head_dim
    seq = lax.axis_index("seq")
    head = lax.axis_index("head")
    bit_of = [lax.rem(seq // (1 << j), 2) for j in range(bits)]
    partner_of = [seq + (1 << j) - 2 * (1 << j) * bit_of[j] for j in range(bits)]

    def weight_copy(chunk):
        return pltpu.make_async_copy(
            w_ref.at[:, :, pl.ds(pl.multiple_of(chunk * width, width), width)],
            w_vm.at[chunk],
            w_sem.at[chunk],
        )

    own = pltpu.make_async_copy(act_ref, acts.at[0], act_sem)
    own.start()
    weight_copy(0).start()
    cot_copy = pltpu.make_async_copy(cot_ref, cot, cot_sem)
    cot_copy.start()

    barrier = pltpu.get_barrier_semaphore()
    for r in range(1, n_head):
        pl.semaphore_signal(
            barrier, inc=1, device_id=(seq, lax.rem(head + r, n_head)), device_id_type=MESH
        )
    for j in range(bits):
        pl.semaphore_signal(barrier, inc=1, device_id=(partner_of[j], head), device_id_type=MESH)
    pl.semaphore_wait(barrier, n_head - 1 + bits)

    def act_copy(r):
        return pltpu.make_async_remote_copy(
            src_ref=act_ref,
            dst_ref=acts.at[r],
            send_sem=act_send_sem.at[r],
            recv_sem=act_recv_sem.at[r],
            device_id=(seq, lax.rem(head + r, n_head)),
            device_id_type=MESH,
        )

    for r in range(1, n_head):
        act_copy(r).start()
    for chunk in range(1, chunks):
        weight_copy(chunk).start()

    levels = lw_ref.shape[0]
    for h in range(heads):
        table = jnp.concatenate(
            [lw_ref[level, h : h + 1, :] * (scale * level_factor(level)) for level in range(levels)]
            + [jnp.zeros((1, block), F32)] * (-levels % 8),
            0,
        )
        wcol[h] = table.T

    def s_copy(stage, chunk):
        return pltpu.make_async_remote_copy(
            src_ref=s_send.at[stage, chunk],
            dst_ref=s_recv.at[stage, chunk],
            send_sem=s_send_sem.at[stage, chunk],
            recv_sem=s_recv_sem.at[stage, chunk],
            device_id=(partner_of[stage], head),
            device_id_type=MESH,
        )

    def r_copy(stage, chunk):
        return pltpu.make_async_remote_copy(
            src_ref=r_send.at[stage, chunk],
            dst_ref=r_recv.at[stage, chunk],
            send_sem=r_send_sem.at[stage, chunk],
            recv_sem=r_recv_sem.at[stage, chunk],
            device_id=(partner_of[bits - 1 - stage], head),
            device_id_type=MESH,
        )

    top = bit_of[bits - 1]

    def start_stage(stage, chunk):
        def send_s():
            s_send[stage, chunk] = group[chunk].astype(BF16)
            s_copy(stage, chunk).start()

        def send_r():
            bit = bits - 1 - stage
            term = rgrad[chunk, :, bit]
            if stage == 0:
                r_send[stage, chunk] = term.astype(BF16)
            else:
                flag = bit_of[bit].astype(F32)
                r_send[stage, chunk] = (moving[chunk] + flag * term).astype(BF16)
            r_copy(stage, chunk).start()

        if stage == bits - 1:
            pl.when(top == 0)(send_s)
        else:
            send_s()
        if stage == 0:
            pl.when(top == 1)(send_r)
        else:
            send_r()

    def finish_stage(stage, chunk):
        rows = pl.ds(stage * head_dim, head_dim)

        if stage == bits - 1:

            @pl.when(top == 1)
            def _():
                s_copy(stage, chunk).wait_recv()
                upper[chunk, :, rows, :] = s_recv[stage, chunk]

            @pl.when(top == 0)
            def _():
                upper[chunk, :, rows, :] = jnp.zeros((per, head_dim, head_dim), BF16)

        else:
            s_copy(stage, chunk).wait_recv()
            got = s_recv[stage, chunk].astype(F32)
            upper[chunk, :, rows, :] = (got * bit_of[stage].astype(F32)).astype(BF16)
            group[chunk] += got

        if stage == 0:

            @pl.when(top == 0)
            def _():
                r_copy(stage, chunk).wait_recv()
                moving[chunk] = r_recv[stage, chunk].astype(F32)

            @pl.when(top == 1)
            def _():
                moving[chunk] = jnp.zeros((per, head_dim, head_dim), F32)

        else:
            r_copy(stage, chunk).wait_recv()
            moving[chunk] += r_recv[stage, chunk].astype(F32)

    def tick(time):
        for stage in range(bits + 1):
            chunk = time - stage

            @pl.when((chunk >= 0) & (chunk < chunks))
            def _():
                if stage > 0:
                    finish_stage(stage - 1, chunk)
                if stage < bits:
                    start_stage(stage, chunk)

    own.wait()
    offsets = [
        pl.multiple_of(lax.rem(head + n_head - r, n_head) * features, features)
        for r in range(n_head)
    ]

    def project(chunk, _):
        weight_copy(chunk).wait()

        @pl.when(chunk == 0)
        def _():
            cot_copy.wait()
            for r in range(1, n_head):
                act_copy(r).wait_recv()

        for c in (1, 2, 0):
            total = dot_nn(acts[0], w_vm[chunk, c, pl.ds(offsets[0], features), :])
            for r in range(1, n_head):
                total += dot_nn(acts[r], w_vm[chunk, c, pl.ds(offsets[r], features), :])
            total = total.astype(BF16)
            for i in range(per):
                qkv[c, chunk * per + i] = total[:, i * head_dim : (i + 1) * head_dim]
        for i in range(per):
            h = chunk * per + i
            group[chunk, i] = dot_tn(qkv[1, h], qkv[2, h])
            query = qkv[0, h].astype(F32)
            columns = wcol[h]
            for j in range(bits):
                level = block_bits + 1 + j
                wq[h, :, j * head_dim : (j + 1) * head_dim] = (
                    query * columns[:, level : level + 1]
                ).astype(BF16)
            lanes = pl.ds(pl.multiple_of(h * head_dim, head_dim), head_dim)
            grads = dot_tn(cot[:, lanes], wq[h])
            for j in range(bits):
                rgrad[chunk, i, j] = grads[:, j * head_dim : (j + 1) * head_dim]
        tick(chunk)
        return 0

    lax.fori_loop(0, chunks, project, 0)

    tile = min(2 * head_dim, block)
    leaf = min(head_dim, tile)
    tiles = block // tile
    row_ids = lax.broadcasted_iota(jnp.int32, (leaf, leaf), 0)
    col_ids = lax.broadcasted_iota(jnp.int32, (leaf, leaf), 1)
    differ = jnp.bitwise_xor(row_ids, col_ids)
    leaf_level = jnp.zeros((leaf, leaf), jnp.int32)
    for shift in range(leaf.bit_length() - 1):
        leaf_level = leaf_level + (differ >= (1 << shift)).astype(jnp.int32)
    leaf_level = jnp.where(col_ids <= row_ids, leaf_level, -1)

    def attend(h):
        lanes = pl.ds(pl.multiple_of(h * head_dim, head_dim), head_dim)
        columns = wcol[h]
        for b in range(tiles):
            first = b * tile
            query = qkv[0, h, first:, :]
            key = qkv[1, h, first : first + tile, :]
            value = qkv[2, h, first : first + tile, :]
            cotangent = cot[first:, lanes]
            mask = [diagonal_mask(columns, first, tile, leaf, (leaf_level, differ))]
            for a in range(b + 1, tiles):
                level = tile.bit_length() - 1 + (a ^ b).bit_length()
                column = columns[a * tile : (a + 1) * tile, level : level + 1]
                mask.append(jnp.broadcast_to(column, (tile, tile)))
            mask = jnp.concatenate(mask, 0) if len(mask) > 1 else mask[0]
            attn = (dot_nt(query, key) * mask).astype(BF16)
            grads = (dot_nt(cotangent, value) * mask).astype(BF16)
            out_part = dot_nn(attn, value)
            dq_part = dot_nn(grads, key)
            if b == 0:
                inner[0, h] = out_part
                inner[1, h] = dq_part
            else:
                inner[0, h, first:, :] += out_part
                inner[1, h, first:, :] += dq_part
            inner[2, h, first : first + tile, :] = dot_tn(grads, query)
            inner[3, h, first : first + tile, :] = dot_tn(attn, cotangent)

    def middle(chunk, _):
        tick(chunks + chunk)
        for i in range(per):
            attend(chunk * per + i)
        return 0

    lax.fori_loop(0, chunks, middle, 0)
    for time in range(2 * chunks, chunks + bits):
        tick(time)

    def cross(chunk, _):
        for i in range(per):
            h = chunk * per + i
            lanes = pl.ds(pl.multiple_of(h * head_dim, head_dim), head_dim)
            columns = wcol[h]
            states = upper[chunk, i]
            out_ref[:, lanes] = (inner[0, h] + dot_nn(wq[h], states)).astype(BF16)
            back = dot_nt(cot[:, lanes], states)
            total = inner[1, h]
            for j in range(bits):
                level = block_bits + 1 + j
                total += (
                    back[:, j * head_dim : (j + 1) * head_dim] * columns[:, level : level + 1]
                )
            dq_ref[:, lanes] = total.astype(BF16)
            suffix = moving[chunk, i].astype(BF16)
            dk_ref[:, lanes] = (inner[2, h] + dot_nn(qkv[2, h], suffix)).astype(BF16)
            dv_ref[:, lanes] = (inner[3, h] + dot_nt(qkv[1, h], suffix)).astype(BF16)
        return 0

    lax.fori_loop(0, chunks, cross, 0)

    for r in range(1, n_head):
        act_copy(r).wait_send()

    def drain(chunk, _):
        for stage in range(bits):
            if stage == bits - 1:
                pl.when(top == 0)(lambda: s_copy(stage, chunk).wait_send())
            else:
                s_copy(stage, chunk).wait_send()
            if stage == 0:
                pl.when(top == 1)(lambda: r_copy(stage, chunk).wait_send())
            else:
                r_copy(stage, chunk).wait_send()
        return 0

    lax.fori_loop(0, chunks, drain, 0)


def on_device(n_seq, n_head, activations, w_proj, level_weight, grad_out):
    block, features = activations.shape
    width = w_proj.shape[2]
    heads = level_weight.shape[1]
    head_dim = width // heads
    per = 2 if heads % 2 == 0 else 1
    chunks = heads // per
    bits = n_seq.bit_length() - 1
    levels = level_weight.shape[2]
    padded = levels + (-levels % 8)
    dims = (n_seq, n_head, heads, head_dim, block, features, per)
    square = (head_dim, head_dim)
    result = jax.ShapeDtypeStruct((block, width), BF16)
    dma = pltpu.SemaphoreType.DMA
    any_spec = pl.BlockSpec(memory_space=pl.ANY)
    vmem_spec = pl.BlockSpec(memory_space=pltpu.VMEM)
    return pl.pallas_call(
        functools.partial(kernel, dims),
        out_shape=[result] * 4,
        in_specs=[any_spec, any_spec, vmem_spec, any_spec],
        out_specs=[vmem_spec] * 4,
        scratch_shapes=[
            pltpu.VMEM((n_head, block, features), BF16),
            pltpu.VMEM((chunks, 3, w_proj.shape[1], per * head_dim), BF16),
            pltpu.VMEM((block, width), BF16),
            pltpu.VMEM((heads, block, padded), F32),
            pltpu.VMEM((3, heads, block, head_dim), BF16),
            pltpu.VMEM((heads, block, bits * head_dim), BF16),
            pltpu.VMEM((chunks, per) + square, F32),
            pltpu.VMEM((chunks, per, bits) + square, F32),
            pltpu.VMEM((chunks, per) + square, F32),
            pltpu.VMEM((bits, chunks, per) + square, BF16),
            pltpu.VMEM((bits, chunks, per) + square, BF16),
            pltpu.VMEM((bits, chunks, per) + square, BF16),
            pltpu.VMEM((bits, chunks, per) + square, BF16),
            pltpu.VMEM((chunks, per, bits * head_dim, head_dim), BF16),
            pltpu.VMEM((4, heads, block, head_dim), F32),
            dma,
            dma,
            dma((chunks,)),
            dma((n_head,)),
            dma((n_head,)),
            dma((bits, chunks)),
            dma((bits, chunks)),
            dma((bits, chunks)),
            dma((bits, chunks)),
        ],
        compiler_params=pltpu.CompilerParams(
            collective_id=0, has_side_effects=True, vmem_limit_bytes=56 * 2**20
        ),
    )(activations, w_proj, jnp.transpose(level_weight, (2, 1, 0)), grad_out)


def solution(mesh):
    in_specs = (P("seq", "head"), P(None, None, "head"), P("seq", "head", None), P("seq", "head"))
    out_specs = (P("seq", "head"), P("seq", "head"), P("seq", "head"), P("seq", "head"))
    return jax.shard_map(
        functools.partial(on_device, mesh.shape["seq"], mesh.shape["head"]),
        mesh=mesh,
        in_specs=in_specs,
        out_specs=out_specs,
        check_vma=False,
    )
```

```python
import functools

import jax
import jax.numpy as jnp
from jax import lax
from jax.experimental import pallas as pl
from jax.experimental.pallas import tpu as pltpu
from jax.sharding import PartitionSpec as P

MESH = pl.DeviceIdType.MESH
F32 = jnp.float32
BF16 = jnp.bfloat16


def dot_nn(a, b):
    return lax.dot_general(a, b, (((1,), (0,)), ((), ())), preferred_element_type=F32)


def dot_nt(a, b):
    return lax.dot_general(a, b, (((1,), (1,)), ((), ())), preferred_element_type=F32)


def dot_tn(a, b):
    return lax.dot_general(a, b, (((0,), (0,)), ((), ())), preferred_element_type=F32)


def level_factor(level):
    return 2.0 ** (-0.5 * (max(level, 1) - 1))


def diagonal_mask(rows, start, size, leaf, leaf_level):
    if size == leaf:
        total = jnp.zeros((leaf, leaf), F32)
        for level in range(leaf.bit_length()):
            row = rows[level : level + 1, start : start + leaf]
            total = jnp.where(leaf_level == level, row, total)
        return total
    half = size // 2
    early = diagonal_mask(rows, start, half, leaf, leaf_level)
    late = diagonal_mask(rows, start + half, half, leaf, leaf_level)
    level = half.bit_length()
    side = jnp.broadcast_to(
        rows[level : level + 1, start + half : start + size], (half, half)
    )
    return jnp.concatenate(
        [
            jnp.concatenate([early, side], 1),
            jnp.concatenate([jnp.zeros((half, half), F32), late], 1),
        ],
        0,
    )


def state_kernel(
    dims,
    act_ref,
    w_ref,
    lw_ref,
    cot_ref,
    rows_out,
    qt_out,
    ct_out,
    k_out,
    v_out,
    inner_t_out,
    inner_out,
    upper_out,
    suffix_out,
    acts,
    w_vm,
    cot,
    partial,
    rows_vm,
    qkv,
    cots,
    qt_vm,
    kt_vm,
    vt_vm,
    ct_vm,
    group,
    rgrad,
    moving,
    suffix,
    s_send,
    s_recv,
    r_send,
    r_recv,
    upper,
    inner_t,
    inner,
    act_sem,
    cot_sem,
    w_sem,
    act_send_sem,
    act_recv_sem,
    s_send_sem,
    s_recv_sem,
    r_send_sem,
    r_recv_sem,
    rows_sem,
    early_sem,
    inner_sem,
    late_sem,
):
    n_seq, n_head, heads, head_dim, block, features, per = dims
    chunks = heads // per
    bits = n_seq.bit_length() - 1
    block_bits = block.bit_length() - 1
    scale = head_dim**-0.5
    width = per * head_dim
    seq = lax.axis_index("seq")
    head = lax.axis_index("head")
    bit_of = [lax.rem(seq // (1 << j), 2) for j in range(bits)]
    partner_of = [seq + (1 << j) - 2 * (1 << j) * bit_of[j] for j in range(bits)]

    def weight_copy(chunk):
        return pltpu.make_async_copy(
            w_ref.at[:, :, pl.ds(pl.multiple_of(chunk * width, width), width)],
            w_vm.at[chunk],
            w_sem.at[chunk],
        )

    own = pltpu.make_async_copy(act_ref, acts.at[0], act_sem)
    own.start()
    weight_copy(0).start()
    cot_copy = pltpu.make_async_copy(cot_ref, cot, cot_sem)
    cot_copy.start()

    barrier = pltpu.get_barrier_semaphore()
    for r in range(1, n_head):
        pl.semaphore_signal(
            barrier, inc=1, device_id=(seq, lax.rem(head + r, n_head)), device_id_type=MESH
        )
    for j in range(bits):
        pl.semaphore_signal(barrier, inc=1, device_id=(partner_of[j], head), device_id_type=MESH)
    pl.semaphore_wait(barrier, n_head - 1 + bits)

    def act_copy(r):
        return pltpu.make_async_remote_copy(
            src_ref=act_ref,
            dst_ref=acts.at[r],
            send_sem=act_send_sem.at[r],
            recv_sem=act_recv_sem.at[r],
            device_id=(seq, lax.rem(head + r, n_head)),
            device_id_type=MESH,
        )

    for r in range(1, n_head):
        act_copy(r).start()
    for chunk in range(1, chunks):
        weight_copy(chunk).start()

    levels = lw_ref.shape[0]
    for h in range(heads):
        rows_vm[h] = jnp.concatenate(
            [lw_ref[level, h : h + 1, :] * (scale * level_factor(level)) for level in range(levels)]
            + [jnp.zeros((1, block), F32)] * (-levels % 8),
            0,
        )
    rows_copy = pltpu.make_async_copy(rows_vm, rows_out, rows_sem)
    rows_copy.start()

    def early_copies(chunk):
        pairs = ((qt_vm, qt_out), (ct_vm, ct_out), (qkv.at[1], k_out), (qkv.at[2], v_out))
        heads_of = pl.ds(chunk * per, per)
        return [
            pltpu.make_async_copy(source.at[heads_of], target.at[heads_of], early_sem.at[n, chunk])
            for n, (source, target) in enumerate(pairs)
        ]

    def inner_copies(chunk):
        heads_of = pl.ds(chunk * per, per)
        pairs = ((inner_t, inner_t_out), (inner, inner_out))
        return [
            pltpu.make_async_copy(
                source.at[:, heads_of], target.at[:, heads_of], inner_sem.at[n, chunk]
            )
            for n, (source, target) in enumerate(pairs)
        ]

    def late_copies(chunk):
        pairs = ((upper, upper_out), (suffix, suffix_out))
        return [
            pltpu.make_async_copy(source.at[chunk], target.at[chunk], late_sem.at[n, chunk])
            for n, (source, target) in enumerate(pairs)
        ]

    def s_copy(stage, chunk):
        return pltpu.make_async_remote_copy(
            src_ref=s_send.at[stage, chunk],
            dst_ref=s_recv.at[stage, chunk],
            send_sem=s_send_sem.at[stage, chunk],
            recv_sem=s_recv_sem.at[stage, chunk],
            device_id=(partner_of[stage], head),
            device_id_type=MESH,
        )

    def r_copy(stage, chunk):
        return pltpu.make_async_remote_copy(
            src_ref=r_send.at[stage, chunk],
            dst_ref=r_recv.at[stage, chunk],
            send_sem=r_send_sem.at[stage, chunk],
            recv_sem=r_recv_sem.at[stage, chunk],
            device_id=(partner_of[bits - 1 - stage], head),
            device_id_type=MESH,
        )

    top = bit_of[bits - 1]

    def start_stage(stage, chunk):
        def send_s():
            s_send[stage, chunk] = group[chunk].astype(BF16)
            s_copy(stage, chunk).start()

        def send_r():
            bit = bits - 1 - stage
            term = rgrad[chunk, :, bit]
            if stage == 0:
                r_send[stage, chunk] = term.astype(BF16)
            else:
                flag = bit_of[bit].astype(F32)
                r_send[stage, chunk] = (moving[chunk] + flag * term).astype(BF16)
            r_copy(stage, chunk).start()

        if stage == bits - 1:
            pl.when(top == 0)(send_s)
        else:
            send_s()
        if stage == 0:
            pl.when(top == 1)(send_r)
        else:
            send_r()

    def finish_stage(stage, chunk):

        if stage == bits - 1:

            @pl.when(top == 1)
            def _():
                s_copy(stage, chunk).wait_recv()
                upper[chunk, :, stage] = s_recv[stage, chunk]

            @pl.when(top == 0)
            def _():
                upper[chunk, :, stage] = jnp.zeros((per, head_dim, head_dim), BF16)

        else:
            s_copy(stage, chunk).wait_recv()
            got = s_recv[stage, chunk].astype(F32)
            upper[chunk, :, stage] = (got * bit_of[stage].astype(F32)).astype(BF16)
            group[chunk] += got

        if stage == 0:

            @pl.when(top == 0)
            def _():
                r_copy(stage, chunk).wait_recv()
                moving[chunk] = r_recv[stage, chunk].astype(F32)

            @pl.when(top == 1)
            def _():
                moving[chunk] = jnp.zeros((per, head_dim, head_dim), F32)

        else:
            r_copy(stage, chunk).wait_recv()
            moving[chunk] += r_recv[stage, chunk].astype(F32)

    def tick(time):
        for stage in range(bits + 1):
            chunk = time - stage

            @pl.when((chunk >= 0) & (chunk < chunks))
            def _():
                if stage > 0:
                    finish_stage(stage - 1, chunk)
                if stage < bits:
                    start_stage(stage, chunk)
                else:
                    suffix[chunk] = moving[chunk].astype(BF16)
                    for copy in late_copies(chunk):
                        copy.start()

    own.wait()
    offsets = [
        pl.multiple_of(lax.rem(head + n_head - r, n_head) * features, features)
        for r in range(n_head)
    ]

    def project(chunk, _):
        weight_copy(chunk).wait()
        for c in (1, 2, 0):
            partial[c] = dot_nn(acts[0], w_vm[chunk, c, pl.ds(offsets[0], features), :])

        @pl.when(chunk == 0)
        def _():
            cot_copy.wait()
            for r in range(1, n_head):
                act_copy(r).wait_recv()

        for c in (1, 2, 0):
            total = partial[c]
            for r in range(1, n_head):
                total += dot_nn(acts[r], w_vm[chunk, c, pl.ds(offsets[r], features), :])
            total = total.astype(BF16)
            for i in range(per):
                qkv[c, chunk * per + i] = total[:, i * head_dim : (i + 1) * head_dim]
        for i in range(per):
            h = chunk * per + i
            lanes = pl.ds(pl.multiple_of(h * head_dim, head_dim), head_dim)
            cotangent = cot[:, lanes]
            cots[h] = cotangent
            key_t = qkv[1, h].T
            group[chunk, i] = dot_nn(key_t, qkv[2, h])
            query_t = qkv[0, h].T
            wide = query_t.astype(F32)
            weights = rows_vm[h]
            for j in range(bits):
                level = block_bits + 1 + j
                weighted = (wide * weights[level : level + 1, :]).astype(BF16)
                rgrad[chunk, i, j] = dot_nn(weighted, cotangent)
            kt_vm[h] = key_t
            qt_vm[h] = query_t
            vt_vm[h] = qkv[2, h].T
            ct_vm[h] = cotangent.T
        for copy in early_copies(chunk):
            copy.start()
        tick(chunk)
        return 0

    lax.fori_loop(0, chunks, project, 0)

    tile = min(2 * head_dim, block)
    leaf = min(head_dim, tile)
    tiles = block // tile
    early_ids = lax.broadcasted_iota(jnp.int32, (leaf, leaf), 0)
    late_ids = lax.broadcasted_iota(jnp.int32, (leaf, leaf), 1)
    differ = jnp.bitwise_xor(early_ids, late_ids)
    leaf_level = jnp.zeros((leaf, leaf), jnp.int32)
    for shift in range(leaf.bit_length() - 1):
        leaf_level = leaf_level + (differ >= (1 << shift)).astype(jnp.int32)
    leaf_level = jnp.where(early_ids <= late_ids, leaf_level, -1)

    def attend(h):
        weights = rows_vm[h]
        for a in range(tiles):
            here = slice(a * tile, (a + 1) * tile)
            end = (a + 1) * tile
            mask = []
            for b in range(a):
                level = tile.bit_length() - 1 + (a ^ b).bit_length()
                mask.append(jnp.broadcast_to(weights[level : level + 1, here], (tile, tile)))
            mask.append(diagonal_mask(weights, a * tile, tile, leaf, leaf_level))
            mask = jnp.concatenate(mask, 0) if a else mask[0]
            attn = (dot_nn(qkv[1, h, :end, :], qt_vm[h, :, here]) * mask).astype(BF16)
            grads = (dot_nn(qkv[2, h, :end, :], ct_vm[h, :, here]) * mask).astype(BF16)
            inner_t[0, h, :, here] = dot_nn(vt_vm[h, :, :end], attn)
            inner_t[1, h, :, here] = dot_nn(kt_vm[h, :, :end], grads)
            dk_part = dot_nn(grads, qkv[0, h, here, :])
            dv_part = dot_nn(attn, cots[h, here, :])
            if a:
                inner[0, h, : a * tile, :] += dk_part[: a * tile]
                inner[1, h, : a * tile, :] += dv_part[: a * tile]
            inner[0, h, here, :] = dk_part[a * tile :]
            inner[1, h, here, :] = dv_part[a * tile :]

    def middle(chunk, _):
        attend(chunk * per)
        pl.when(chunk < chunks - 1)(lambda: tick(chunks + chunk))
        for i in range(1, per):
            attend(chunk * per + i)
        for copy in inner_copies(chunk):
            copy.start()
        return 0

    lax.fori_loop(0, chunks, middle, 0)
    for time in range(2 * chunks - 1, chunks + bits):
        tick(time)

    for r in range(1, n_head):
        act_copy(r).wait_send()

    def drain(chunk, _):
        for stage in range(bits):
            if stage == bits - 1:
                pl.when(top == 0)(lambda: s_copy(stage, chunk).wait_send())
            else:
                s_copy(stage, chunk).wait_send()
            if stage == 0:
                pl.when(top == 1)(lambda: r_copy(stage, chunk).wait_send())
            else:
                r_copy(stage, chunk).wait_send()
        for copy in early_copies(chunk) + inner_copies(chunk) + late_copies(chunk):
            copy.wait()
        return 0

    lax.fori_loop(0, chunks, drain, 0)
    rows_copy.wait()


def cross_kernel(
    dims,
    rows_ref,
    qt_ref,
    ct_ref,
    k_ref,
    v_ref,
    inner_t_ref,
    inner_ref,
    upper_ref,
    suffix_ref,
    out_ref,
    dq_ref,
    dk_ref,
    dv_ref,
):
    n_seq, n_head, heads, head_dim, block, features, per = dims
    bits = n_seq.bit_length() - 1
    block_bits = block.bit_length() - 1
    for i in range(per):
        lanes = slice(i * head_dim, (i + 1) * head_dim)
        weights = rows_ref[i]

        def weighted(transposed):
            wide = transposed.astype(F32)
            parts = []
            for j in range(bits):
                level = block_bits + 1 + j
                parts.append((wide * weights[level : level + 1, :]).astype(BF16))
            return jnp.concatenate(parts, 0)

        states = upper_ref[0, i]
        tall = states.reshape(bits * head_dim, head_dim)
        wide = jnp.concatenate([states[j] for j in range(bits)], 1)
        out_t = inner_t_ref[0, i] + dot_nn(tall.T, weighted(qt_ref[i]))
        dq_t = inner_t_ref[1, i] + dot_nn(wide, weighted(ct_ref[i]))
        out_ref[:, lanes] = out_t.astype(BF16).T
        dq_ref[:, lanes] = dq_t.astype(BF16).T
        suffix = suffix_ref[0, i]
        dk_ref[:, lanes] = (inner_ref[0, i] + dot_nt(v_ref[i], suffix)).astype(BF16)
        dv_ref[:, lanes] = (inner_ref[1, i] + dot_nn(k_ref[i], suffix)).astype(BF16)


def on_device(n_seq, n_head, activations, w_proj, level_weight, grad_out):
    block, features = activations.shape
    width = w_proj.shape[2]
    heads = level_weight.shape[1]
    head_dim = width // heads
    per = 2 if heads % 2 == 0 else 1
    chunks = heads // per
    bits = n_seq.bit_length() - 1
    levels = level_weight.shape[2]
    padded = levels + (-levels % 8)
    dims = (n_seq, n_head, heads, head_dim, block, features, per)
    square = (head_dim, head_dim)
    tall = (block, head_dim)
    flat = (head_dim, block)
    dma = pltpu.SemaphoreType.DMA
    any_spec = pl.BlockSpec(memory_space=pl.ANY)
    vmem_spec = pl.BlockSpec(memory_space=pltpu.VMEM)
    between = [
        ((heads, padded, block), F32),
        ((heads,) + flat, BF16),
        ((heads,) + flat, BF16),
        ((heads,) + tall, BF16),
        ((heads,) + tall, BF16),
        ((2, heads) + flat, F32),
        ((2, heads) + tall, F32),
        ((chunks, per, bits) + square, BF16),
        ((chunks, per) + square, BF16),
    ]
    parts = pl.pallas_call(
        functools.partial(state_kernel, dims),
        out_shape=[jax.ShapeDtypeStruct(shape, dtype) for shape, dtype in between],
        in_specs=[any_spec, any_spec, vmem_spec, any_spec],
        out_specs=[any_spec] * len(between),
        scratch_shapes=[
            pltpu.VMEM((n_head, block, features), BF16),
            pltpu.VMEM((chunks, 3, w_proj.shape[1], per * head_dim), BF16),
            pltpu.VMEM((block, width), BF16),
            pltpu.VMEM((3, block, per * head_dim), F32),
            pltpu.VMEM((heads, padded, block), F32),
            pltpu.VMEM((3, heads) + tall, BF16),
            pltpu.VMEM((heads,) + tall, BF16),
            pltpu.VMEM((heads,) + flat, BF16),
            pltpu.VMEM((heads,) + flat, BF16),
            pltpu.VMEM((heads,) + flat, BF16),
            pltpu.VMEM((heads,) + flat, BF16),
            pltpu.VMEM((chunks, per) + square, F32),
            pltpu.VMEM((chunks, per, bits) + square, F32),
            pltpu.VMEM((chunks, per) + square, F32),
            pltpu.VMEM((chunks, per) + square, BF16),
            pltpu.VMEM((bits, chunks, per) + square, BF16),
            pltpu.VMEM((bits, chunks, per) + square, BF16),
            pltpu.VMEM((bits, chunks, per) + square, BF16),
            pltpu.VMEM((bits, chunks, per) + square, BF16),
            pltpu.VMEM((chunks, per, bits) + square, BF16),
            pltpu.VMEM((2, heads) + flat, F32),
            pltpu.VMEM((2, heads) + tall, F32),
            dma,
            dma,
            dma((chunks,)),
            dma((n_head,)),
            dma((n_head,)),
            dma((bits, chunks)),
            dma((bits, chunks)),
            dma((bits, chunks)),
            dma((bits, chunks)),
            dma,
            dma((4, chunks)),
            dma((2, chunks)),
            dma((2, chunks)),
        ],
        compiler_params=pltpu.CompilerParams(
            collective_id=0, has_side_effects=True, vmem_limit_bytes=56 * 2**20
        ),
    )(activations, w_proj, jnp.transpose(level_weight, (2, 1, 0)), grad_out)

    def by_head(shape):
        return pl.BlockSpec((per,) + shape[1:], lambda n: (n,) + (0,) * (len(shape) - 1))

    def by_pair(shape):
        return pl.BlockSpec((2, per) + shape[2:], lambda n: (0, n) + (0,) * (len(shape) - 2))

    def by_chunk(shape):
        return pl.BlockSpec((1,) + shape[1:], lambda n: (n,) + (0,) * (len(shape) - 1))

    makers = [by_head] * 5 + [by_pair] * 2 + [by_chunk] * 2
    return pl.pallas_call(
        functools.partial(cross_kernel, dims),
        grid=(chunks,),
        out_shape=[jax.ShapeDtypeStruct((block, width), BF16)] * 4,
        in_specs=[maker(shape) for maker, (shape, _) in zip(makers, between)],
        out_specs=[pl.BlockSpec((block, per * head_dim), lambda n: (0, n))] * 4,
        compiler_params=pltpu.CompilerParams(vmem_limit_bytes=40 * 2**20),
    )(*parts)


def solution(mesh):
    in_specs = (P("seq", "head"), P(None, None, "head"), P("seq", "head", None), P("seq", "head"))
    out_specs = (P("seq", "head"), P("seq", "head"), P("seq", "head"), P("seq", "head"))
    return jax.shard_map(
        functools.partial(on_device, mesh.shape["seq"], mesh.shape["head"]),
        mesh=mesh,
        in_specs=in_specs,
        out_specs=out_specs,
        check_vma=False,
    )
```

```python
import functools

import jax
import jax.numpy as jnp
from jax import lax
from jax.experimental import pallas as pl
from jax.experimental.pallas import tpu as pltpu
from jax.sharding import PartitionSpec as P

MESH = pl.DeviceIdType.MESH
F32 = jnp.float32
BF16 = jnp.bfloat16


def dot_nn(a, b):
    return lax.dot_general(a, b, (((1,), (0,)), ((), ())), preferred_element_type=F32)


def dot_nt(a, b):
    return lax.dot_general(a, b, (((1,), (1,)), ((), ())), preferred_element_type=F32)


def dot_tn(a, b):
    return lax.dot_general(a, b, (((0,), (0,)), ((), ())), preferred_element_type=F32)


def level_factor(level):
    return 2.0 ** (-0.5 * (max(level, 1) - 1))


def diagonal_mask(rows, start, size, leaf, leaf_level):
    if size == leaf:
        total = jnp.zeros((leaf, leaf), F32)
        for level in range(leaf.bit_length()):
            row = rows[level : level + 1, start : start + leaf]
            total = jnp.where(leaf_level == level, row, total)
        return total
    half = size // 2
    early = diagonal_mask(rows, start, half, leaf, leaf_level)
    late = diagonal_mask(rows, start + half, half, leaf, leaf_level)
    level = half.bit_length()
    side = jnp.broadcast_to(
        rows[level : level + 1, start + half : start + size], (half, half)
    )
    return jnp.concatenate(
        [
            jnp.concatenate([early, side], 1),
            jnp.concatenate([jnp.zeros((half, half), F32), late], 1),
        ],
        0,
    )


def state_kernel(
    dims,
    act_ref,
    w_ref,
    lw_ref,
    cot_ref,
    rows_out,
    qt_out,
    ct_out,
    k_out,
    v_out,
    inner_t_out,
    inner_out,
    upper_out,
    suffix_out,
    acts,
    w_vm,
    cot,
    partial,
    rows_vm,
    qkv,
    cots,
    qt_vm,
    kt_vm,
    vt_vm,
    ct_vm,
    group,
    rgrad,
    moving,
    suffix,
    s_send,
    s_recv,
    r_send,
    r_recv,
    upper,
    inner_t,
    inner,
    act_sem,
    cot_sem,
    w_sem,
    act_send_sem,
    act_recv_sem,
    s_send_sem,
    s_recv_sem,
    r_send_sem,
    r_recv_sem,
    rows_sem,
    early_sem,
    inner_sem,
    late_sem,
):
    n_seq, n_head, heads, head_dim, block, features, per = dims
    chunks = heads // per
    bits = n_seq.bit_length() - 1
    block_bits = block.bit_length() - 1
    scale = head_dim**-0.5
    width = per * head_dim
    seq = lax.axis_index("seq")
    head = lax.axis_index("head")
    bit_of = [lax.rem(seq // (1 << j), 2) for j in range(bits)]
    top = bits - 1
    below = bits - 2
    reach = 1 << below
    quarter = seq // reach
    partner_of = [seq + (1 << j) - 2 * (1 << j) * bit_of[j] for j in range(bits)]

    def weight_copy(chunk):
        return pltpu.make_async_copy(
            w_ref.at[:, :, pl.ds(pl.multiple_of(chunk * width, width), width)],
            w_vm.at[chunk],
            w_sem.at[chunk],
        )

    own = pltpu.make_async_copy(act_ref, acts.at[0], act_sem)
    own.start()
    weight_copy(0).start()
    cot_copy = pltpu.make_async_copy(cot_ref, cot, cot_sem)
    cot_copy.start()

    barrier = pltpu.get_barrier_semaphore()
    for r in range(1, n_head):
        pl.semaphore_signal(
            barrier, inc=1, device_id=(seq, lax.rem(head + r, n_head)), device_id_type=MESH
        )
    for j in range(top):
        pl.semaphore_signal(barrier, inc=1, device_id=(partner_of[j], head), device_id_type=MESH)

    @pl.when(quarter == 1)
    def _():
        for step in (1, 2):
            other = seq + step * reach
            pl.semaphore_signal(barrier, inc=1, device_id=(other, head), device_id_type=MESH)

    @pl.when(quarter >= 2)
    def _():
        other = seq - (quarter - 1) * reach
        pl.semaphore_signal(barrier, inc=1, device_id=(other, head), device_id_type=MESH)

    peers = n_head - 1 + top
    pl.when(quarter == 0)(lambda: pl.semaphore_wait(barrier, peers))
    pl.when(quarter == 1)(lambda: pl.semaphore_wait(barrier, peers + 2))
    pl.when(quarter >= 2)(lambda: pl.semaphore_wait(barrier, peers + 1))

    def act_copy(r):
        return pltpu.make_async_remote_copy(
            src_ref=act_ref,
            dst_ref=acts.at[r],
            send_sem=act_send_sem.at[r],
            recv_sem=act_recv_sem.at[r],
            device_id=(seq, lax.rem(head + r, n_head)),
            device_id_type=MESH,
        )

    for r in range(1, n_head):
        act_copy(r).start()
    for chunk in range(1, chunks):
        weight_copy(chunk).start()

    levels = lw_ref.shape[0]
    for h in range(heads):
        rows_vm[h] = jnp.concatenate(
            [lw_ref[level, h : h + 1, :] * (scale * level_factor(level)) for level in range(levels)]
            + [jnp.zeros((1, block), F32)] * (-levels % 8),
            0,
        )
    rows_copy = pltpu.make_async_copy(rows_vm, rows_out, rows_sem)
    rows_copy.start()

    def early_copies(chunk):
        pairs = ((qt_vm, qt_out), (ct_vm, ct_out), (qkv.at[1], k_out), (qkv.at[2], v_out))
        heads_of = pl.ds(chunk * per, per)
        return [
            pltpu.make_async_copy(source.at[heads_of], target.at[heads_of], early_sem.at[n, chunk])
            for n, (source, target) in enumerate(pairs)
        ]

    def inner_copies(chunk):
        heads_of = pl.ds(chunk * per, per)
        pairs = ((inner_t, inner_t_out), (inner, inner_out))
        return [
            pltpu.make_async_copy(
                source.at[:, heads_of], target.at[:, heads_of], inner_sem.at[n, chunk]
            )
            for n, (source, target) in enumerate(pairs)
        ]

    def late_copies(chunk):
        pairs = ((upper, upper_out), (suffix, suffix_out))
        return [
            pltpu.make_async_copy(source.at[chunk], target.at[chunk], late_sem.at[n, chunk])
            for n, (source, target) in enumerate(pairs)
        ]

    def s_copy(stage, chunk, target, slot):
        return pltpu.make_async_remote_copy(
            src_ref=s_send.at[stage, chunk],
            dst_ref=s_recv.at[stage, chunk],
            send_sem=s_send_sem.at[slot, chunk],
            recv_sem=s_recv_sem.at[stage, chunk],
            device_id=(target, head),
            device_id_type=MESH,
        )

    def r_copy(stage, chunk, target, slot):
        return pltpu.make_async_remote_copy(
            src_ref=r_send.at[stage, chunk],
            dst_ref=r_recv.at[slot, chunk],
            send_sem=r_send_sem.at[stage, chunk],
            recv_sem=r_recv_sem.at[slot, chunk],
            device_id=(target, head),
            device_id_type=MESH,
        )

    def s_copies(stage, chunk):
        if stage == top:
            return [
                (quarter == 1, s_copy(stage, chunk, seq + reach, stage)),
                (quarter == 1, s_copy(stage, chunk, seq + 2 * reach, bits)),
            ]
        copy = s_copy(stage, chunk, partner_of[stage], stage)
        return [(bit_of[below] == 0 if stage == below else None, copy)]

    def r_copies(stage, chunk):
        if stage == 0:
            return [
                (quarter == 2, r_copy(stage, chunk, seq - reach, stage)),
                (quarter == 3, r_copy(stage, chunk, seq - 2 * reach, bits)),
            ]
        copy = r_copy(stage, chunk, partner_of[top - stage], stage)
        return [(bit_of[below] == 1 if stage == 1 else None, copy)]

    def only_if(condition, action):
        if condition is None:
            action()
        else:
            pl.when(condition)(action)

    def start_s(stage, chunk):
        s_send[stage, chunk] = group[chunk].astype(BF16)
        for condition, copy in s_copies(stage, chunk):
            only_if(condition, copy.start)

    def start_r(stage, chunk):
        bit = top - stage
        term = rgrad[chunk, :, bit]
        if stage > 0:
            term = moving[chunk] + bit_of[bit].astype(F32) * term
        r_send[stage, chunk] = term.astype(BF16)
        for condition, copy in r_copies(stage, chunk):
            only_if(condition, copy.start)

    def finish_s(stage, chunk):
        if stage < below:
            s_copy(stage, chunk, partner_of[stage], stage).wait_recv()
            got = s_recv[stage, chunk].astype(F32)
            upper[chunk, :, stage] = (got * bit_of[stage].astype(F32)).astype(BF16)
            group[chunk] += got
            return
        takes = bit_of[stage] == 1

        @pl.when(takes)
        def _():
            s_copy(stage, chunk, partner_of[stage], stage).wait_recv()
            got = s_recv[stage, chunk]
            upper[chunk, :, stage] = got
            if stage == below:
                group[chunk] += got.astype(F32)

        @pl.when(jnp.logical_not(takes))
        def _():
            upper[chunk, :, stage] = jnp.zeros((per, head_dim, head_dim), BF16)

    def finish_r(stage, chunk):
        if stage == 0:

            @pl.when(quarter == 1)
            def _():
                r_copy(0, chunk, seq + reach, 0).wait_recv()
                r_copy(0, chunk, seq + 2 * reach, bits).wait_recv()
                moving[chunk] = r_recv[0, chunk].astype(F32) + r_recv[bits, chunk].astype(F32)

            @pl.when(quarter != 1)
            def _():
                moving[chunk] = jnp.zeros((per, head_dim, head_dim), F32)

            return

        def take():
            r_copy(stage, chunk, partner_of[top - stage], stage).wait_recv()
            moving[chunk] += r_recv[stage, chunk].astype(F32)

        only_if(bit_of[below] == 0 if stage == 1 else None, take)

    def tick(time, start, finish, last):
        for stage in range(bits + 1):
            chunk = time - stage

            @pl.when((chunk >= 0) & (chunk < chunks))
            def _():
                if stage > 0:
                    finish(stage - 1, chunk)
                if stage < bits:
                    start(stage, chunk)
                else:
                    last(chunk)

    def last_s(chunk):
        late_copies(chunk)[0].start()

    def last_r(chunk):
        suffix[chunk] = moving[chunk].astype(BF16)
        late_copies(chunk)[1].start()

    def tick_s(time):
        tick(time, start_s, finish_s, last_s)

    def tick_r(time):
        tick(time, start_r, finish_r, last_r)

    own.wait()
    offsets = [
        pl.multiple_of(lax.rem(head + n_head - r, n_head) * features, features)
        for r in range(n_head)
    ]

    def project(chunk, _):
        weight_copy(chunk).wait()
        for c in (1, 2, 0):
            partial[c] = dot_nn(acts[0], w_vm[chunk, c, pl.ds(offsets[0], features), :])

        @pl.when(chunk == 0)
        def _():
            cot_copy.wait()
            for r in range(1, n_head):
                act_copy(r).wait_recv()

        def finish_projection(c):
            total = partial[c]
            for r in range(1, n_head):
                total += dot_nn(acts[r], w_vm[chunk, c, pl.ds(offsets[r], features), :])
            total = total.astype(BF16)
            for i in range(per):
                qkv[c, chunk * per + i] = total[:, i * head_dim : (i + 1) * head_dim]

        finish_projection(1)
        finish_projection(2)
        for i in range(per):
            h = chunk * per + i
            key_t = qkv[1, h].T
            group[chunk, i] = dot_nn(key_t, qkv[2, h])
            kt_vm[h] = key_t
            vt_vm[h] = qkv[2, h].T
        tick_s(chunk)
        finish_projection(0)
        for i in range(per):
            h = chunk * per + i
            lanes = pl.ds(pl.multiple_of(h * head_dim, head_dim), head_dim)
            cotangent = cot[:, lanes]
            cots[h] = cotangent
            query_t = qkv[0, h].T
            wide = query_t.astype(F32)
            weights = rows_vm[h]
            for j in range(bits):
                level = block_bits + 1 + j
                weighted = (wide * weights[level : level + 1, :]).astype(BF16)
                rgrad[chunk, i, j] = dot_nn(weighted, cotangent)
            qt_vm[h] = query_t
            ct_vm[h] = cotangent.T
        for copy in early_copies(chunk):
            copy.start()
        tick_r(chunk)
        return 0

    lax.fori_loop(0, chunks, project, 0)

    tile = min(2 * head_dim, block)
    leaf = min(head_dim, tile)
    tiles = block // tile
    early_ids = lax.broadcasted_iota(jnp.int32, (leaf, leaf), 0)
    late_ids = lax.broadcasted_iota(jnp.int32, (leaf, leaf), 1)
    differ = jnp.bitwise_xor(early_ids, late_ids)
    leaf_level = jnp.zeros((leaf, leaf), jnp.int32)
    for shift in range(leaf.bit_length() - 1):
        leaf_level = leaf_level + (differ >= (1 << shift)).astype(jnp.int32)
    leaf_level = jnp.where(early_ids <= late_ids, leaf_level, -1)

    def attend(h):
        weights = rows_vm[h]
        for a in range(tiles):
            here = slice(a * tile, (a + 1) * tile)
            end = (a + 1) * tile
            mask = []
            for b in range(a):
                level = tile.bit_length() - 1 + (a ^ b).bit_length()
                mask.append(jnp.broadcast_to(weights[level : level + 1, here], (tile, tile)))
            mask.append(diagonal_mask(weights, a * tile, tile, leaf, leaf_level))
            mask = jnp.concatenate(mask, 0) if a else mask[0]
            attn = (dot_nn(qkv[1, h, :end, :], qt_vm[h, :, here]) * mask).astype(BF16)
            grads = (dot_nn(qkv[2, h, :end, :], ct_vm[h, :, here]) * mask).astype(BF16)
            inner_t[0, h, :, here] = dot_nn(vt_vm[h, :, :end], attn)
            inner_t[1, h, :, here] = dot_nn(kt_vm[h, :, :end], grads)
            dk_part = dot_nn(grads, qkv[0, h, here, :])
            dv_part = dot_nn(attn, cots[h, here, :])
            if a:
                inner[0, h, : a * tile, :] += dk_part[: a * tile]
                inner[1, h, : a * tile, :] += dv_part[: a * tile]
            inner[0, h, here, :] = dk_part[a * tile :]
            inner[1, h, here, :] = dv_part[a * tile :]

    def middle(chunk, _):
        attend(chunk * per)
        pl.when(chunk < chunks - 1)(lambda: tick_s(chunks + chunk))
        for i in range(1, per):
            attend(chunk * per + i)
        pl.when(chunk < chunks - 1)(lambda: tick_r(chunks + chunk))
        for copy in inner_copies(chunk):
            copy.start()
        return 0

    lax.fori_loop(0, chunks, middle, 0)
    for time in range(2 * chunks - 1, chunks + bits):
        tick_s(time)
        tick_r(time)

    for r in range(1, n_head):
        act_copy(r).wait_send()

    def drain(chunk, _):
        for stage in range(bits):
            for condition, copy in s_copies(stage, chunk) + r_copies(stage, chunk):
                only_if(condition, copy.wait_send)
        for copy in early_copies(chunk) + inner_copies(chunk) + late_copies(chunk):
            copy.wait()
        return 0

    lax.fori_loop(0, chunks, drain, 0)
    rows_copy.wait()


def cross_kernel(
    dims,
    rows_ref,
    qt_ref,
    ct_ref,
    k_ref,
    v_ref,
    inner_t_ref,
    inner_ref,
    upper_ref,
    suffix_ref,
    out_ref,
    dq_ref,
    dk_ref,
    dv_ref,
):
    n_seq, n_head, heads, head_dim, block, features, per = dims
    bits = n_seq.bit_length() - 1
    block_bits = block.bit_length() - 1
    for i in range(per):
        lanes = slice(i * head_dim, (i + 1) * head_dim)
        weights = rows_ref[i]

        def weighted(transposed):
            wide = transposed.astype(F32)
            parts = []
            for j in range(bits):
                level = block_bits + 1 + j
                parts.append((wide * weights[level : level + 1, :]).astype(BF16))
            return jnp.concatenate(parts, 0)

        states = upper_ref[0, i]
        tall = states.reshape(bits * head_dim, head_dim)
        wide = jnp.concatenate([states[j] for j in range(bits)], 1)
        out_t = inner_t_ref[0, i] + dot_nn(tall.T, weighted(qt_ref[i]))
        dq_t = inner_t_ref[1, i] + dot_nn(wide, weighted(ct_ref[i]))
        out_ref[:, lanes] = out_t.astype(BF16).T
        dq_ref[:, lanes] = dq_t.astype(BF16).T
        suffix = suffix_ref[0, i]
        dk_ref[:, lanes] = (inner_ref[0, i] + dot_nt(v_ref[i], suffix)).astype(BF16)
        dv_ref[:, lanes] = (inner_ref[1, i] + dot_nn(k_ref[i], suffix)).astype(BF16)


def on_device(n_seq, n_head, activations, w_proj, level_weight, grad_out):
    block, features = activations.shape
    width = w_proj.shape[2]
    heads = level_weight.shape[1]
    head_dim = width // heads
    per = 2 if heads % 2 == 0 else 1
    chunks = heads // per
    bits = n_seq.bit_length() - 1
    levels = level_weight.shape[2]
    padded = levels + (-levels % 8)
    dims = (n_seq, n_head, heads, head_dim, block, features, per)
    square = (head_dim, head_dim)
    tall = (block, head_dim)
    flat = (head_dim, block)
    dma = pltpu.SemaphoreType.DMA
    any_spec = pl.BlockSpec(memory_space=pl.ANY)
    vmem_spec = pl.BlockSpec(memory_space=pltpu.VMEM)
    between = [
        ((heads, padded, block), F32),
        ((heads,) + flat, BF16),
        ((heads,) + flat, BF16),
        ((heads,) + tall, BF16),
        ((heads,) + tall, BF16),
        ((2, heads) + flat, F32),
        ((2, heads) + tall, F32),
        ((chunks, per, bits) + square, BF16),
        ((chunks, per) + square, BF16),
    ]
    parts = pl.pallas_call(
        functools.partial(state_kernel, dims),
        out_shape=[jax.ShapeDtypeStruct(shape, dtype) for shape, dtype in between],
        in_specs=[any_spec, any_spec, vmem_spec, any_spec],
        out_specs=[any_spec] * len(between),
        scratch_shapes=[
            pltpu.VMEM((n_head, block, features), BF16),
            pltpu.VMEM((chunks, 3, w_proj.shape[1], per * head_dim), BF16),
            pltpu.VMEM((block, width), BF16),
            pltpu.VMEM((3, block, per * head_dim), F32),
            pltpu.VMEM((heads, padded, block), F32),
            pltpu.VMEM((3, heads) + tall, BF16),
            pltpu.VMEM((heads,) + tall, BF16),
            pltpu.VMEM((heads,) + flat, BF16),
            pltpu.VMEM((heads,) + flat, BF16),
            pltpu.VMEM((heads,) + flat, BF16),
            pltpu.VMEM((heads,) + flat, BF16),
            pltpu.VMEM((chunks, per) + square, F32),
            pltpu.VMEM((chunks, per, bits) + square, F32),
            pltpu.VMEM((chunks, per) + square, F32),
            pltpu.VMEM((chunks, per) + square, BF16),
            pltpu.VMEM((bits, chunks, per) + square, BF16),
            pltpu.VMEM((bits, chunks, per) + square, BF16),
            pltpu.VMEM((bits, chunks, per) + square, BF16),
            pltpu.VMEM((bits + 1, chunks, per) + square, BF16),
            pltpu.VMEM((chunks, per, bits) + square, BF16),
            pltpu.VMEM((2, heads) + flat, F32),
            pltpu.VMEM((2, heads) + tall, F32),
            dma,
            dma,
            dma((chunks,)),
            dma((n_head,)),
            dma((n_head,)),
            dma((bits + 1, chunks)),
            dma((bits, chunks)),
            dma((bits, chunks)),
            dma((bits + 1, chunks)),
            dma,
            dma((4, chunks)),
            dma((2, chunks)),
            dma((2, chunks)),
        ],
        compiler_params=pltpu.CompilerParams(
            collective_id=0, has_side_effects=True, vmem_limit_bytes=56 * 2**20
        ),
    )(activations, w_proj, jnp.transpose(level_weight, (2, 1, 0)), grad_out)

    def by_head(shape):
        return pl.BlockSpec((per,) + shape[1:], lambda n: (n,) + (0,) * (len(shape) - 1))

    def by_pair(shape):
        return pl.BlockSpec((2, per) + shape[2:], lambda n: (0, n) + (0,) * (len(shape) - 2))

    def by_chunk(shape):
        return pl.BlockSpec((1,) + shape[1:], lambda n: (n,) + (0,) * (len(shape) - 1))

    makers = [by_head] * 5 + [by_pair] * 2 + [by_chunk] * 2
    return pl.pallas_call(
        functools.partial(cross_kernel, dims),
        grid=(chunks,),
        out_shape=[jax.ShapeDtypeStruct((block, width), BF16)] * 4,
        in_specs=[maker(shape) for maker, (shape, _) in zip(makers, between)],
        out_specs=[pl.BlockSpec((block, per * head_dim), lambda n: (0, n))] * 4,
        compiler_params=pltpu.CompilerParams(vmem_limit_bytes=60 * 2**20),
    )(*parts)


def solution(mesh):
    in_specs = (P("seq", "head"), P(None, None, "head"), P("seq", "head", None), P("seq", "head"))
    out_specs = (P("seq", "head"), P("seq", "head"), P("seq", "head"), P("seq", "head"))
    return jax.shard_map(
        functools.partial(on_device, mesh.shape["seq"], mesh.shape["head"]),
        mesh=mesh,
        in_specs=in_specs,
        out_specs=out_specs,
        check_vma=False,
    )
```

```python
import functools

import jax
import jax.numpy as jnp
from jax import lax
from jax.experimental import pallas as pl
from jax.experimental.pallas import tpu as pltpu
from jax.sharding import PartitionSpec as P

MESH = pl.DeviceIdType.MESH
F32 = jnp.float32
BF16 = jnp.bfloat16


def dot_nn(a, b):
    return lax.dot_general(a, b, (((1,), (0,)), ((), ())), preferred_element_type=F32)


def dot_nt(a, b):
    return lax.dot_general(a, b, (((1,), (1,)), ((), ())), preferred_element_type=F32)


def dot_tn(a, b):
    return lax.dot_general(a, b, (((0,), (0,)), ((), ())), preferred_element_type=F32)


def level_factor(level):
    return 2.0 ** (-0.5 * (max(level, 1) - 1))


def diagonal_mask(rows, start, size, leaf, leaf_level):
    if size == leaf:
        total = jnp.zeros((leaf, leaf), F32)
        for level in range(leaf.bit_length()):
            row = rows[level : level + 1, start : start + leaf]
            total = jnp.where(leaf_level == level, row, total)
        return total
    half = size // 2
    early = diagonal_mask(rows, start, half, leaf, leaf_level)
    late = diagonal_mask(rows, start + half, half, leaf, leaf_level)
    level = half.bit_length()
    side = jnp.broadcast_to(
        rows[level : level + 1, start + half : start + size], (half, half)
    )
    return jnp.concatenate(
        [
            jnp.concatenate([early, side], 1),
            jnp.concatenate([jnp.zeros((half, half), F32), late], 1),
        ],
        0,
    )


def state_kernel(
    dims,
    act_ref,
    w_ref,
    lw_ref,
    cot_ref,
    out_ref,
    dq_ref,
    dk_ref,
    dv_ref,
    acts,
    w_vm,
    cot,
    partial,
    rows_vm,
    qkv,
    cots,
    qt_vm,
    kt_vm,
    vt_vm,
    ct_vm,
    group,
    rgrad,
    moving,
    s_send,
    s_recv,
    r_send,
    r_recv,
    upper,
    inner_t,
    inner,
    finals,
    act_sem,
    cot_sem,
    w_sem,
    act_send_sem,
    act_recv_sem,
    s_send_sem,
    s_recv_sem,
    r_send_sem,
    r_recv_sem,
    final_sem,
):
    n_seq, n_head, heads, head_dim, block, features, per = dims
    chunks = heads // per
    bits = n_seq.bit_length() - 1
    block_bits = block.bit_length() - 1
    scale = head_dim**-0.5
    width = per * head_dim
    seq = lax.axis_index("seq")
    head = lax.axis_index("head")
    bit_of = [lax.rem(seq // (1 << j), 2) for j in range(bits)]
    top = bits - 1
    below = bits - 2
    reach = 1 << below
    quarter = seq // reach
    partner_of = [seq + (1 << j) - 2 * (1 << j) * bit_of[j] for j in range(bits)]

    def weight_copy(c, chunk):
        return pltpu.make_async_copy(
            w_ref.at[c, :, pl.ds(pl.multiple_of(chunk * width, width), width)],
            w_vm.at[chunk, c],
            w_sem.at[c, chunk],
        )

    own = pltpu.make_async_copy(act_ref, acts.at[0], act_sem)
    own.start()
    weight_copy(1, 0).start()
    weight_copy(2, 0).start()
    cot_copy = pltpu.make_async_copy(cot_ref, cot, cot_sem)
    cot_copy.start()

    barrier = pltpu.get_barrier_semaphore()
    for r in range(1, n_head):
        pl.semaphore_signal(
            barrier, inc=1, device_id=(seq, lax.rem(head + r, n_head)), device_id_type=MESH
        )
    for j in range(top):
        pl.semaphore_signal(barrier, inc=1, device_id=(partner_of[j], head), device_id_type=MESH)

    @pl.when((quarter == 1) | (quarter == 2))
    def _():
        other = seq + reach * (3 - 2 * quarter)
        pl.semaphore_signal(barrier, inc=1, device_id=(other, head), device_id_type=MESH)

    peers = n_head - 1 + top
    middle_half = (quarter == 1) | (quarter == 2)
    pl.when(middle_half)(lambda: pl.semaphore_wait(barrier, peers + 1))
    pl.when(jnp.logical_not(middle_half))(lambda: pl.semaphore_wait(barrier, peers))

    def act_copy(r):
        return pltpu.make_async_remote_copy(
            src_ref=act_ref,
            dst_ref=acts.at[r],
            send_sem=act_send_sem.at[r],
            recv_sem=act_recv_sem.at[r],
            device_id=(seq, lax.rem(head + r, n_head)),
            device_id_type=MESH,
        )

    for r in range(1, n_head):
        act_copy(r).start()
    for chunk in range(1, chunks):
        weight_copy(1, chunk).start()
        weight_copy(2, chunk).start()
    for chunk in range(chunks):
        weight_copy(0, chunk).start()

    levels = lw_ref.shape[0]
    for h in range(heads):
        rows_vm[h] = jnp.concatenate(
            [lw_ref[level, h : h + 1, :] * (scale * level_factor(level)) for level in range(levels)]
            + [jnp.zeros((1, block), F32)] * (-levels % 8),
            0,
        )
    stages = bits + 1

    def s_way(stage):
        if stage < below:
            return None, None, partner_of[stage]
        if stage == below:
            return bit_of[below] == 0, bit_of[below] == 1, partner_of[below]
        return quarter == stage - below, quarter == stage - below + 1, None

    def r_way(stage):
        if stage < 2:
            return quarter == 3 - stage, quarter == 2 - stage, None
        bit = bits - stage
        if stage == 2:
            return bit_of[below] == 1, bit_of[below] == 0, partner_of[below]
        return None, None, partner_of[bit]

    def remote(send, recv, send_sem, recv_sem, stage, chunk, target):
        return pltpu.make_async_remote_copy(
            src_ref=send.at[stage, chunk],
            dst_ref=recv.at[stage, chunk],
            send_sem=send_sem.at[stage, chunk],
            recv_sem=recv_sem.at[stage, chunk],
            device_id=(target, head),
            device_id_type=MESH,
        )

    def s_copy(stage, chunk):
        target = s_way(stage)[2]
        target = seq + reach if target is None else target
        return remote(s_send, s_recv, s_send_sem, s_recv_sem, stage, chunk, target)

    def r_copy(stage, chunk):
        target = r_way(stage)[2]
        target = seq - reach if target is None else target
        return remote(r_send, r_recv, r_send_sem, r_recv_sem, stage, chunk, target)

    def only_if(condition, action):
        if condition is None:
            action()
        else:
            pl.when(condition)(action)

    def start_s(stage, chunk):
        def send():
            s_send[stage, chunk] = group[chunk].astype(BF16)
            s_copy(stage, chunk).start()

        only_if(s_way(stage)[0], send)

    def start_r(stage, chunk):
        bit = top if stage < 2 else bits - stage

        def send():
            term = rgrad[chunk, :, bit]
            if stage == 1:
                term = term + moving[chunk]
            if stage >= 2:
                term = moving[chunk] + bit_of[bit].astype(F32) * term
            r_send[stage, chunk] = term.astype(BF16)
            r_copy(stage, chunk).start()

        only_if(r_way(stage)[0], send)

    zero = (per, head_dim, head_dim)

    def finish_s(stage, chunk):
        def take():
            s_copy(stage, chunk).wait_recv()
            got = s_recv[stage, chunk]
            if stage < below:
                flag = bit_of[stage].astype(F32)
                upper[chunk, :, stage] = (got.astype(F32) * flag).astype(BF16)
            else:
                upper[chunk, :, min(stage, top)] = got
            if stage <= below:
                group[chunk] += got.astype(F32)
            if stage == top:
                group[chunk] = got.astype(F32)

        if stage == below:

            @pl.when(bit_of[below] == 0)
            def _():
                upper[chunk, :, below] = jnp.zeros(zero, BF16)

        if stage == top:

            @pl.when(quarter < 2)
            def _():
                upper[chunk, :, top] = jnp.zeros(zero, BF16)

        only_if(s_way(stage)[1], take)

    def finish_r(stage, chunk):
        def take():
            r_copy(stage, chunk).wait_recv()
            got = r_recv[stage, chunk].astype(F32)
            if stage < 2:
                moving[chunk] = got
            else:
                moving[chunk] += got

        if stage == 0:
            moving[chunk] = jnp.zeros(zero, F32)
        if stage == 2:

            @pl.when(quarter == 2)
            def _():
                moving[chunk] = jnp.zeros(zero, F32)

        only_if(r_way(stage)[1], take)

    lag = 2
    heads_end = 2 * chunks + heads
    s_base, r_base = chunks, chunks + lag
    last_slot = r_base + lag * bits + chunks - 1
    crossing_inside = all(
        r_base + lag * bits + c >= 2 * chunks + per * (c + 1) - 1 for c in range(chunks)
    )

    def tick(slot, low, high):
        for stage in range(stages):
            for base, finish, start, is_r in (
                (s_base, finish_s, start_s, False),
                (r_base, finish_r, start_r, True),
            ):
                first = base + lag * stage
                if first > high or first + chunks - 1 < low:
                    continue
                chunk = slot - first

                @pl.when((chunk >= 0) & (chunk < chunks))
                def _():
                    finish(stage, chunk)
                    if stage < bits:
                        start(stage + 1, chunk)
                    elif is_r and crossing_inside:
                        cross(chunk)

    def final_copies(chunk):
        lanes = pl.ds(pl.multiple_of(chunk * width, width), width)
        return [
            pltpu.make_async_copy(
                finals.at[n, :, lanes], target.at[:, lanes], final_sem.at[n, chunk]
            )
            for n, target in enumerate((out_ref, dq_ref, dk_ref, dv_ref))
        ]

    def cross(chunk):
        for i in range(per):
            h = chunk * per + i
            lanes = pl.ds(pl.multiple_of(h * head_dim, head_dim), head_dim)
            weights = rows_vm[h]

            def weighted(transposed):
                full = transposed.astype(F32)
                parts = []
                for j in range(bits):
                    level = block_bits + 1 + j
                    parts.append((full * weights[level : level + 1, :]).astype(BF16))
                return jnp.concatenate(parts, 0)

            states = upper[chunk, i]
            tall = states.reshape(bits * head_dim, head_dim)
            wide = jnp.concatenate([states[j] for j in range(bits)], 1)
            out_t = inner_t[0, h] + dot_nn(tall.T, weighted(qt_vm[h]))
            dq_t = inner_t[1, h] + dot_nn(wide, weighted(ct_vm[h]))
            finals[0, :, lanes] = out_t.astype(BF16).T
            finals[1, :, lanes] = dq_t.astype(BF16).T
            suffix = moving[chunk, i].astype(BF16)
            finals[2, :, lanes] = (inner[0, h] + dot_nt(qkv[2, h], suffix)).astype(BF16)
            finals[3, :, lanes] = (inner[1, h] + dot_nn(qkv[1, h], suffix)).astype(BF16)
        for copy in final_copies(chunk):
            copy.start()

    own.wait()
    offsets = [
        pl.multiple_of(lax.rem(head + n_head - r, n_head) * features, features)
        for r in range(n_head)
    ]

    def own_part(c, chunk):
        weight_copy(c, chunk).wait()
        partial[c] = dot_nn(acts[0], w_vm[chunk, c, pl.ds(offsets[0], features), :])

    def finish_projection(c, chunk):
        total = partial[c]
        for r in range(1, n_head):
            total += dot_nn(acts[r], w_vm[chunk, c, pl.ds(offsets[r], features), :])
        total = total.astype(BF16)
        for i in range(per):
            qkv[c, chunk * per + i] = total[:, i * head_dim : (i + 1) * head_dim]

    def project_kv(chunk, _):
        own_part(1, chunk)
        own_part(2, chunk)

        @pl.when(chunk == 0)
        def _():
            for r in range(1, n_head):
                act_copy(r).wait_recv()

        finish_projection(1, chunk)
        finish_projection(2, chunk)
        for i in range(per):
            h = chunk * per + i
            key_t = qkv[1, h].T
            group[chunk, i] = dot_nn(key_t, qkv[2, h])
            kt_vm[h] = key_t
            vt_vm[h] = qkv[2, h].T
        start_s(0, chunk)
        return 0

    lax.fori_loop(0, chunks, project_kv, 0)
    cot_copy.wait()

    def project_q(chunk, _):
        own_part(0, chunk)
        finish_projection(0, chunk)
        for i in range(per):
            h = chunk * per + i
            lanes = pl.ds(pl.multiple_of(h * head_dim, head_dim), head_dim)
            cotangent = cot[:, lanes]
            cots[h] = cotangent
            query_t = qkv[0, h].T
            wide = query_t.astype(F32)
            weights = rows_vm[h]
            for j in range(bits):
                level = block_bits + 1 + j
                weighted = (wide * weights[level : level + 1, :]).astype(BF16)
                rgrad[chunk, i, j] = dot_nn(weighted, cotangent)
            qt_vm[h] = query_t
            ct_vm[h] = cotangent.T
        start_r(0, chunk)
        tick(chunks + chunk, chunks, 2 * chunks - 1)
        return 0

    lax.fori_loop(0, chunks, project_q, 0)

    tile = min(2 * head_dim, block)
    leaf = min(head_dim, tile)
    tiles = block // tile
    early_ids = lax.broadcasted_iota(jnp.int32, (leaf, leaf), 0)
    late_ids = lax.broadcasted_iota(jnp.int32, (leaf, leaf), 1)
    differ = jnp.bitwise_xor(early_ids, late_ids)
    leaf_level = jnp.zeros((leaf, leaf), jnp.int32)
    for shift in range(leaf.bit_length() - 1):
        leaf_level = leaf_level + (differ >= (1 << shift)).astype(jnp.int32)
    leaf_level = jnp.where(early_ids <= late_ids, leaf_level, -1)

    def attend(h):
        weights = rows_vm[h]
        for a in range(tiles):
            here = slice(a * tile, (a + 1) * tile)
            end = (a + 1) * tile
            mask = []
            for b in range(a):
                level = tile.bit_length() - 1 + (a ^ b).bit_length()
                mask.append(jnp.broadcast_to(weights[level : level + 1, here], (tile, tile)))
            mask.append(diagonal_mask(weights, a * tile, tile, leaf, leaf_level))
            mask = jnp.concatenate(mask, 0) if a else mask[0]
            attn = (dot_nn(qkv[1, h, :end, :], qt_vm[h, :, here]) * mask).astype(BF16)
            grads = (dot_nn(qkv[2, h, :end, :], ct_vm[h, :, here]) * mask).astype(BF16)
            inner_t[0, h, :, here] = dot_nn(vt_vm[h, :, :end], attn)
            inner_t[1, h, :, here] = dot_nn(kt_vm[h, :, :end], grads)
            dk_part = dot_nn(grads, qkv[0, h, here, :])
            dv_part = dot_nn(attn, cots[h, here, :])
            if a:
                inner[0, h, : a * tile, :] += dk_part[: a * tile]
                inner[1, h, : a * tile, :] += dv_part[: a * tile]
            inner[0, h, here, :] = dk_part[a * tile :]
            inner[1, h, here, :] = dv_part[a * tile :]

    def middle(h, _):
        attend(h)
        tick(2 * chunks + h, 2 * chunks, heads_end - 1)
        return 0

    lax.fori_loop(0, heads, middle, 0)

    def settle(slot, _):
        tick(slot, heads_end, last_slot)
        return 0

    if last_slot >= heads_end:
        lax.fori_loop(heads_end, last_slot + 1, settle, 0)
    if not crossing_inside:

        def cross_one(chunk, _):
            cross(chunk)
            return 0

        lax.fori_loop(0, chunks, cross_one, 0)

    for r in range(1, n_head):
        act_copy(r).wait_send()

    def drain(chunk, _):
        for stage in range(stages):
            only_if(s_way(stage)[0], lambda: s_copy(stage, chunk).wait_send())
            only_if(r_way(stage)[0], lambda: r_copy(stage, chunk).wait_send())
        for copy in final_copies(chunk):
            copy.wait()
        return 0

    lax.fori_loop(0, chunks, drain, 0)


def hand_over_kernel(pieces, *refs):
    sources, targets, buffers = refs[:4], refs[4:8], refs[8]
    in_sem, out_sem = refs[9:]
    rows = sources[0].shape[0] // pieces
    order = [(n, piece) for piece in range(pieces) for n in range(4)]

    def copies(n, piece):
        part = pl.ds(piece * rows, rows)
        inward = pltpu.make_async_copy(
            sources[n].at[part], buffers.at[n, part], in_sem.at[n, piece]
        )
        outward = pltpu.make_async_copy(
            buffers.at[n, part], targets[n].at[part], out_sem.at[n, piece]
        )
        return inward, outward

    moves = [copies(n, piece) for n, piece in order]
    for inward, _ in moves:
        inward.start()
    for inward, outward in moves:
        inward.wait()
        outward.start()
    for _, outward in moves:
        outward.wait()


def on_device(n_seq, n_head, activations, w_proj, level_weight, grad_out):
    block, features = activations.shape
    width = w_proj.shape[2]
    heads = level_weight.shape[1]
    head_dim = width // heads
    per = 2 if heads % 2 == 0 else 1
    chunks = heads // per
    bits = n_seq.bit_length() - 1
    levels = level_weight.shape[2]
    padded = levels + (-levels % 8)
    dims = (n_seq, n_head, heads, head_dim, block, features, per)
    square = (head_dim, head_dim)
    tall = (block, head_dim)
    flat = (head_dim, block)
    dma = pltpu.SemaphoreType.DMA
    any_spec = pl.BlockSpec(memory_space=pl.ANY)
    vmem_spec = pl.BlockSpec(memory_space=pltpu.VMEM)
    results = [jax.ShapeDtypeStruct((block, width), BF16)] * 4
    parts = pl.pallas_call(
        functools.partial(state_kernel, dims),
        out_shape=results,
        in_specs=[any_spec, any_spec, vmem_spec, any_spec],
        out_specs=[any_spec] * 4,
        scratch_shapes=[
            pltpu.VMEM((n_head, block, features), BF16),
            pltpu.VMEM((chunks, 3, w_proj.shape[1], per * head_dim), BF16),
            pltpu.VMEM((block, width), BF16),
            pltpu.VMEM((3, block, per * head_dim), F32),
            pltpu.VMEM((heads, padded, block), F32),
            pltpu.VMEM((3, heads) + tall, BF16),
            pltpu.VMEM((heads,) + tall, BF16),
            pltpu.VMEM((heads,) + flat, BF16),
            pltpu.VMEM((heads,) + flat, BF16),
            pltpu.VMEM((heads,) + flat, BF16),
            pltpu.VMEM((heads,) + flat, BF16),
            pltpu.VMEM((chunks, per) + square, F32),
            pltpu.VMEM((chunks, per, bits) + square, F32),
            pltpu.VMEM((chunks, per) + square, F32),
            pltpu.VMEM((bits + 1, chunks, per) + square, BF16),
            pltpu.VMEM((bits + 1, chunks, per) + square, BF16),
            pltpu.VMEM((bits + 1, chunks, per) + square, BF16),
            pltpu.VMEM((bits + 1, chunks, per) + square, BF16),
            pltpu.VMEM((chunks, per, bits) + square, BF16),
            pltpu.VMEM((2, heads) + flat, F32),
            pltpu.VMEM((2, heads) + tall, F32),
            pltpu.VMEM((4, block, width), BF16),
            dma,
            dma,
            dma((3, chunks)),
            dma((n_head,)),
            dma((n_head,)),
            dma((bits + 1, chunks)),
            dma((bits + 1, chunks)),
            dma((bits + 1, chunks)),
            dma((bits + 1, chunks)),
            dma((4, chunks)),
        ],
        compiler_params=pltpu.CompilerParams(
            collective_id=0, has_side_effects=True, vmem_limit_bytes=56 * 2**20
        ),
    )(activations, w_proj, jnp.transpose(level_weight, (2, 1, 0)), grad_out)

    pieces = 2 if block % 256 == 0 else 1
    return pl.pallas_call(
        functools.partial(hand_over_kernel, pieces),
        out_shape=results,
        in_specs=[any_spec] * 4,
        out_specs=[any_spec] * 4,
        scratch_shapes=[
            pltpu.VMEM((4, block, width), BF16),
            dma((4, pieces)),
            dma((4, pieces)),
        ],
        compiler_params=pltpu.CompilerParams(vmem_limit_bytes=60 * 2**20),
    )(*parts)


def solution(mesh):
    in_specs = (P("seq", "head"), P(None, None, "head"), P("seq", "head", None), P("seq", "head"))
    out_specs = (P("seq", "head"), P("seq", "head"), P("seq", "head"), P("seq", "head"))
    return jax.shard_map(
        functools.partial(on_device, mesh.shape["seq"], mesh.shape["head"]),
        mesh=mesh,
        in_specs=in_specs,
        out_specs=out_specs,
        check_vma=False,
    )
```

```python
import functools

import jax
import jax.numpy as jnp
from jax import lax
from jax.experimental import pallas as pl
from jax.experimental.pallas import tpu as pltpu
from jax.sharding import PartitionSpec as P

MESH = pl.DeviceIdType.MESH
F32 = jnp.float32
BF16 = jnp.bfloat16


def dot_nn(a, b):
    return lax.dot_general(a, b, (((1,), (0,)), ((), ())), preferred_element_type=F32)


def dot_nt(a, b):
    return lax.dot_general(a, b, (((1,), (1,)), ((), ())), preferred_element_type=F32)


def dot_tn(a, b):
    return lax.dot_general(a, b, (((0,), (0,)), ((), ())), preferred_element_type=F32)


def level_factor(level):
    return 2.0 ** (-0.5 * (max(level, 1) - 1))


def diagonal_mask(rows, start, size, leaf, leaf_level):
    if size == leaf:
        total = jnp.zeros((leaf, leaf), F32)
        for level in range(leaf.bit_length()):
            row = rows[level : level + 1, start : start + leaf]
            total = jnp.where(leaf_level == level, row, total)
        return total
    half = size // 2
    early = diagonal_mask(rows, start, half, leaf, leaf_level)
    late = diagonal_mask(rows, start + half, half, leaf, leaf_level)
    level = half.bit_length()
    side = jnp.broadcast_to(
        rows[level : level + 1, start + half : start + size], (half, half)
    )
    return jnp.concatenate(
        [
            jnp.concatenate([early, side], 1),
            jnp.concatenate([jnp.zeros((half, half), F32), late], 1),
        ],
        0,
    )


def state_kernel(
    dims,
    act_ref,
    w_ref,
    lw_ref,
    cot_ref,
    out_ref,
    dq_ref,
    dk_ref,
    dv_ref,
    acts,
    w_vm,
    cot,
    partial,
    rows_vm,
    qkv,
    cots,
    qt_vm,
    kt_vm,
    vt_vm,
    ct_vm,
    group,
    rgrad,
    moving,
    s_send,
    s_recv,
    r_send,
    r_recv,
    upper,
    inner_t,
    inner,
    finals,
    act_sem,
    cot_sem,
    w_sem,
    act_send_sem,
    act_recv_sem,
    s_send_sem,
    s_recv_sem,
    r_send_sem,
    r_recv_sem,
    final_sem,
):
    n_seq, n_head, heads, head_dim, block, features, per = dims
    chunks = heads // per
    bits = n_seq.bit_length() - 1
    block_bits = block.bit_length() - 1
    scale = head_dim**-0.5
    width = per * head_dim
    seq = lax.axis_index("seq")
    head = lax.axis_index("head")
    bit_of = [lax.rem(seq // (1 << j), 2) for j in range(bits)]
    top = bits - 1
    below = bits - 2
    reach = 1 << below
    quarter = seq // reach
    partner_of = [seq + (1 << j) - 2 * (1 << j) * bit_of[j] for j in range(bits)]

    def weight_copy(c, chunk):
        return pltpu.make_async_copy(
            w_ref.at[c, :, pl.ds(pl.multiple_of(chunk * width, width), width)],
            w_vm.at[chunk, c],
            w_sem.at[c, chunk],
        )

    own_features = pl.ds(pl.multiple_of(head * features, features), features)
    own = pltpu.make_async_copy(act_ref, acts.at[:, own_features], act_sem)
    own.start()
    weight_copy(1, 0).start()
    weight_copy(2, 0).start()
    cot_copy = pltpu.make_async_copy(cot_ref, cot, cot_sem)

    barrier = pltpu.get_barrier_semaphore()
    for r in range(1, n_head):
        pl.semaphore_signal(
            barrier, inc=1, device_id=(seq, lax.rem(head + r, n_head)), device_id_type=MESH
        )
    for j in range(top):
        pl.semaphore_signal(barrier, inc=1, device_id=(partner_of[j], head), device_id_type=MESH)

    @pl.when((quarter == 1) | (quarter == 2))
    def _():
        other = seq + reach * (3 - 2 * quarter)
        pl.semaphore_signal(barrier, inc=1, device_id=(other, head), device_id_type=MESH)

    peers = n_head - 1 + top
    middle_half = (quarter == 1) | (quarter == 2)
    pl.when(middle_half)(lambda: pl.semaphore_wait(barrier, peers + 1))
    pl.when(jnp.logical_not(middle_half))(lambda: pl.semaphore_wait(barrier, peers))

    def act_copy(r):
        return pltpu.make_async_remote_copy(
            src_ref=act_ref,
            dst_ref=acts.at[:, own_features],
            send_sem=act_send_sem.at[r],
            recv_sem=act_recv_sem.at[r],
            device_id=(seq, lax.rem(head + r, n_head)),
            device_id_type=MESH,
        )

    for r in range(1, n_head):
        act_copy(r).start()

    levels = lw_ref.shape[0]
    for h in range(heads):
        rows_vm[h] = jnp.concatenate(
            [lw_ref[level, h : h + 1, :] * (scale * level_factor(level)) for level in range(levels)]
            + [jnp.zeros((1, block), F32)] * (-levels % 8),
            0,
        )
    stages = bits + 1

    def s_way(stage):
        if stage < below:
            return None, None, partner_of[stage]
        if stage == below:
            return bit_of[below] == 0, bit_of[below] == 1, partner_of[below]
        return quarter == stage - below, quarter == stage - below + 1, None

    def r_way(stage):
        if stage < 2:
            return quarter == 3 - stage, quarter == 2 - stage, None
        bit = bits - stage
        if stage == 2:
            return bit_of[below] == 1, bit_of[below] == 0, partner_of[below]
        return None, None, partner_of[bit]

    def remote(send, recv, send_sem, recv_sem, stage, chunk, target):
        return pltpu.make_async_remote_copy(
            src_ref=send.at[stage, chunk],
            dst_ref=recv.at[stage, chunk],
            send_sem=send_sem.at[stage, chunk],
            recv_sem=recv_sem.at[stage, chunk],
            device_id=(target, head),
            device_id_type=MESH,
        )

    def s_copy(stage, chunk):
        target = s_way(stage)[2]
        target = seq + reach if target is None else target
        return remote(s_send, s_recv, s_send_sem, s_recv_sem, stage, chunk, target)

    def r_copy(stage, chunk):
        target = r_way(stage)[2]
        target = seq - reach if target is None else target
        return remote(r_send, r_recv, r_send_sem, r_recv_sem, stage, chunk, target)

    def only_if(condition, action):
        if condition is None:
            action()
        else:
            pl.when(condition)(action)

    def start_s(stage, chunk):
        def send():
            s_send[stage, chunk] = group[chunk].astype(BF16)
            s_copy(stage, chunk).start()

        only_if(s_way(stage)[0], send)

    def start_r(stage, chunk):
        bit = top if stage < 2 else bits - stage

        def send():
            term = rgrad[chunk, :, bit]
            if stage == 1:
                term = term + moving[chunk]
            if stage >= 2:
                term = moving[chunk] + bit_of[bit].astype(F32) * term
            r_send[stage, chunk] = term.astype(BF16)
            r_copy(stage, chunk).start()

        only_if(r_way(stage)[0], send)

    zero = (per, head_dim, head_dim)

    def finish_s(stage, chunk):
        def take():
            s_copy(stage, chunk).wait_recv()
            got = s_recv[stage, chunk]
            if stage < below:
                flag = bit_of[stage].astype(F32)
                upper[chunk, :, stage] = (got.astype(F32) * flag).astype(BF16)
            else:
                upper[chunk, :, min(stage, top)] = got
            if stage <= below:
                group[chunk] += got.astype(F32)
            if stage == top:
                group[chunk] = got.astype(F32)

        if stage == below:

            @pl.when(bit_of[below] == 0)
            def _():
                upper[chunk, :, below] = jnp.zeros(zero, BF16)

        if stage == top:

            @pl.when(quarter < 2)
            def _():
                upper[chunk, :, top] = jnp.zeros(zero, BF16)

        only_if(s_way(stage)[1], take)

    def finish_r(stage, chunk):
        def take():
            r_copy(stage, chunk).wait_recv()
            got = r_recv[stage, chunk].astype(F32)
            if stage < 2:
                moving[chunk] = got
            else:
                moving[chunk] += got

        if stage == 0:
            moving[chunk] = jnp.zeros(zero, F32)
        if stage == 2:

            @pl.when(quarter == 2)
            def _():
                moving[chunk] = jnp.zeros(zero, F32)

        only_if(r_way(stage)[1], take)

    lag = 2
    heads_end = 2 * chunks + heads
    s_base, r_base = chunks, chunks + lag
    last_slot = r_base + lag * bits + chunks - 1
    crossing_inside = all(
        r_base + lag * bits + c >= 2 * chunks + per * (c + 1) - 1 for c in range(chunks)
    )

    def tick(slot, low, high):
        for stage in range(stages):
            for base, finish, start, is_r in (
                (s_base, finish_s, start_s, False),
                (r_base, finish_r, start_r, True),
            ):
                first = base + lag * stage
                if first > high or first + chunks - 1 < low:
                    continue
                chunk = slot - first

                @pl.when((chunk >= 0) & (chunk < chunks))
                def _():
                    finish(stage, chunk)
                    if stage < bits:
                        start(stage + 1, chunk)
                    elif is_r and crossing_inside:
                        cross(chunk)

    def final_copies(chunk):
        lanes = pl.ds(pl.multiple_of(chunk * width, width), width)
        return [
            pltpu.make_async_copy(
                finals.at[n, :, lanes], target.at[:, lanes], final_sem.at[n, chunk]
            )
            for n, target in enumerate((out_ref, dq_ref, dk_ref, dv_ref))
        ]

    def cross(chunk):
        for i in range(per):
            h = chunk * per + i
            lanes = pl.ds(pl.multiple_of(h * head_dim, head_dim), head_dim)
            weights = rows_vm[h]

            def weighted(transposed):
                full = transposed.astype(F32)
                parts = []
                for j in range(bits):
                    level = block_bits + 1 + j
                    parts.append((full * weights[level : level + 1, :]).astype(BF16))
                return jnp.concatenate(parts, 0)

            states = upper[chunk, i]
            tall = states.reshape(bits * head_dim, head_dim)
            wide = jnp.concatenate([states[j] for j in range(bits)], 1)
            out_t = inner_t[0, h] + dot_nn(tall.T, weighted(qt_vm[h]))
            dq_t = inner_t[1, h] + dot_nn(wide, weighted(ct_vm[h]))
            finals[0, :, lanes] = out_t.astype(BF16).T
            finals[1, :, lanes] = dq_t.astype(BF16).T
            suffix = moving[chunk, i].astype(BF16)
            finals[2, :, lanes] = (inner[0, h] + dot_nt(qkv[2, h], suffix)).astype(BF16)
            finals[3, :, lanes] = (inner[1, h] + dot_nn(qkv[1, h], suffix)).astype(BF16)
        for copy in final_copies(chunk):
            copy.start()

    own.wait()
    def keep(c, chunk, total):
        total = total.astype(BF16)
        for i in range(per):
            qkv[c, chunk * per + i] = total[:, i * head_dim : (i + 1) * head_dim]

    def project(c, chunk):
        keep(c, chunk, dot_nn(acts[...], w_vm[chunk, c]))

    def project_kv(chunk, _):
        for c in (1, 2):
            pl.when(chunk + 1 < chunks)(lambda: weight_copy(c, chunk + 1).start())
            weight_copy(c, chunk).wait()

        @pl.when(chunk == 0)
        def _():
            for c in (1, 2):
                partial[c - 1] = dot_nn(acts[:, own_features], w_vm[0, c, own_features, :])
            cot_copy.start()
            for r in range(1, n_head):
                act_copy(r).wait_recv()
            for c in (1, 2):
                total = partial[c - 1]
                for r in range(1, n_head):
                    other = lax.rem(head + n_head - r, n_head)
                    other = pl.ds(pl.multiple_of(other * features, features), features)
                    total += dot_nn(acts[:, other], w_vm[0, c, other, :])
                keep(c, 0, total)

        @pl.when(chunk > 0)
        def _():
            project(1, chunk)
            project(2, chunk)

        pl.when(chunk == chunks - 1)(lambda: weight_copy(0, 0).start())
        for i in range(per):
            h = chunk * per + i
            key_t = qkv[1, h].T
            group[chunk, i] = dot_nn(key_t, qkv[2, h])
            kt_vm[h] = key_t
            vt_vm[h] = qkv[2, h].T
        start_s(0, chunk)
        return 0

    lax.fori_loop(0, chunks, project_kv, 0)
    cot_copy.wait()

    def project_q(chunk, _):
        pl.when(chunk + 1 < chunks)(lambda: weight_copy(0, chunk + 1).start())
        weight_copy(0, chunk).wait()
        project(0, chunk)
        for i in range(per):
            h = chunk * per + i
            lanes = pl.ds(pl.multiple_of(h * head_dim, head_dim), head_dim)
            cotangent = cot[:, lanes]
            cots[h] = cotangent
            query_t = qkv[0, h].T
            wide = query_t.astype(F32)
            weights = rows_vm[h]
            for j in range(bits):
                level = block_bits + 1 + j
                weighted = (wide * weights[level : level + 1, :]).astype(BF16)
                rgrad[chunk, i, j] = dot_nn(weighted, cotangent)
            qt_vm[h] = query_t
            ct_vm[h] = cotangent.T
        start_r(0, chunk)
        tick(chunks + chunk, chunks, 2 * chunks - 1)
        return 0

    lax.fori_loop(0, chunks, project_q, 0)

    tile = min(2 * head_dim, block)
    leaf = min(head_dim, tile)
    tiles = block // tile
    early_ids = lax.broadcasted_iota(jnp.int32, (leaf, leaf), 0)
    late_ids = lax.broadcasted_iota(jnp.int32, (leaf, leaf), 1)
    differ = jnp.bitwise_xor(early_ids, late_ids)
    leaf_level = jnp.zeros((leaf, leaf), jnp.int32)
    for shift in range(leaf.bit_length() - 1):
        leaf_level = leaf_level + (differ >= (1 << shift)).astype(jnp.int32)
    leaf_level = jnp.where(early_ids <= late_ids, leaf_level, -1)

    def attend(h):
        weights = rows_vm[h]
        for a in range(tiles):
            here = slice(a * tile, (a + 1) * tile)
            end = (a + 1) * tile
            mask = []
            for b in range(a):
                level = tile.bit_length() - 1 + (a ^ b).bit_length()
                mask.append(jnp.broadcast_to(weights[level : level + 1, here], (tile, tile)))
            mask.append(diagonal_mask(weights, a * tile, tile, leaf, leaf_level))
            mask = jnp.concatenate(mask, 0) if a else mask[0]
            attn = (dot_nn(qkv[1, h, :end, :], qt_vm[h, :, here]) * mask).astype(BF16)
            grads = (dot_nn(qkv[2, h, :end, :], ct_vm[h, :, here]) * mask).astype(BF16)
            inner_t[0, h, :, here] = dot_nn(vt_vm[h, :, :end], attn)
            inner_t[1, h, :, here] = dot_nn(kt_vm[h, :, :end], grads)
            dk_part = dot_nn(grads, qkv[0, h, here, :])
            dv_part = dot_nn(attn, cots[h, here, :])
            if a:
                inner[0, h, : a * tile, :] += dk_part[: a * tile]
                inner[1, h, : a * tile, :] += dv_part[: a * tile]
            inner[0, h, here, :] = dk_part[a * tile :]
            inner[1, h, here, :] = dv_part[a * tile :]

    def middle(h, _):
        attend(h)
        tick(2 * chunks + h, 2 * chunks, heads_end - 1)
        return 0

    lax.fori_loop(0, heads, middle, 0)

    def settle(slot, _):
        tick(slot, heads_end, last_slot)
        return 0

    if last_slot >= heads_end:
        lax.fori_loop(heads_end, last_slot + 1, settle, 0)
    if not crossing_inside:

        def cross_one(chunk, _):
            cross(chunk)
            return 0

        lax.fori_loop(0, chunks, cross_one, 0)

    for r in range(1, n_head):
        act_copy(r).wait_send()

    def drain(chunk, _):
        for stage in range(stages):
            only_if(s_way(stage)[0], lambda: s_copy(stage, chunk).wait_send())
            only_if(r_way(stage)[0], lambda: r_copy(stage, chunk).wait_send())
        for copy in final_copies(chunk):
            copy.wait()
        return 0

    lax.fori_loop(0, chunks, drain, 0)


def hand_over_kernel(pieces, *refs):
    sources, targets, buffers = refs[:4], refs[4:8], refs[8]
    in_sem, out_sem = refs[9:]
    rows = sources[0].shape[0] // pieces
    order = [(n, piece) for piece in range(pieces) for n in range(4)]

    def copies(n, piece):
        part = pl.ds(piece * rows, rows)
        inward = pltpu.make_async_copy(
            sources[n].at[part], buffers.at[n, part], in_sem.at[n, piece]
        )
        outward = pltpu.make_async_copy(
            buffers.at[n, part], targets[n].at[part], out_sem.at[n, piece]
        )
        return inward, outward

    moves = [copies(n, piece) for n, piece in order]
    for inward, _ in moves:
        inward.start()
    for inward, outward in moves:
        inward.wait()
        outward.start()
    for _, outward in moves:
        outward.wait()


def on_device(n_seq, n_head, activations, w_proj, level_weight, grad_out):
    block, features = activations.shape
    width = w_proj.shape[2]
    heads = level_weight.shape[1]
    head_dim = width // heads
    per = 2 if heads % 2 == 0 else 1
    chunks = heads // per
    bits = n_seq.bit_length() - 1
    levels = level_weight.shape[2]
    padded = levels + (-levels % 8)
    dims = (n_seq, n_head, heads, head_dim, block, features, per)
    square = (head_dim, head_dim)
    tall = (block, head_dim)
    flat = (head_dim, block)
    dma = pltpu.SemaphoreType.DMA
    any_spec = pl.BlockSpec(memory_space=pl.ANY)
    vmem_spec = pl.BlockSpec(memory_space=pltpu.VMEM)
    results = [jax.ShapeDtypeStruct((block, width), BF16)] * 4
    parts = pl.pallas_call(
        functools.partial(state_kernel, dims),
        out_shape=results,
        in_specs=[any_spec, any_spec, vmem_spec, any_spec],
        out_specs=[any_spec] * 4,
        scratch_shapes=[
            pltpu.VMEM((block, n_head * features), BF16),
            pltpu.VMEM((chunks, 3, w_proj.shape[1], per * head_dim), BF16),
            pltpu.VMEM((block, width), BF16),
            pltpu.VMEM((2, block, per * head_dim), F32),
            pltpu.VMEM((heads, padded, block), F32),
            pltpu.VMEM((3, heads) + tall, BF16),
            pltpu.VMEM((heads,) + tall, BF16),
            pltpu.VMEM((heads,) + flat, BF16),
            pltpu.VMEM((heads,) + flat, BF16),
            pltpu.VMEM((heads,) + flat, BF16),
            pltpu.VMEM((heads,) + flat, BF16),
            pltpu.VMEM((chunks, per) + square, F32),
            pltpu.VMEM((chunks, per, bits) + square, F32),
            pltpu.VMEM((chunks, per) + square, F32),
            pltpu.VMEM((bits + 1, chunks, per) + square, BF16),
            pltpu.VMEM((bits + 1, chunks, per) + square, BF16),
            pltpu.VMEM((bits + 1, chunks, per) + square, BF16),
            pltpu.VMEM((bits + 1, chunks, per) + square, BF16),
            pltpu.VMEM((chunks, per, bits) + square, BF16),
            pltpu.VMEM((2, heads) + flat, F32),
            pltpu.VMEM((2, heads) + tall, F32),
            pltpu.VMEM((4, block, width), BF16),
            dma,
            dma,
            dma((3, chunks)),
            dma((n_head,)),
            dma((n_head,)),
            dma((bits + 1, chunks)),
            dma((bits + 1, chunks)),
            dma((bits + 1, chunks)),
            dma((bits + 1, chunks)),
            dma((4, chunks)),
        ],
        compiler_params=pltpu.CompilerParams(
            collective_id=0, has_side_effects=True, vmem_limit_bytes=56 * 2**20
        ),
    )(activations, w_proj, jnp.transpose(level_weight, (2, 1, 0)), grad_out)

    pieces = 2 if block % 256 == 0 else 1
    return pl.pallas_call(
        functools.partial(hand_over_kernel, pieces),
        out_shape=results,
        in_specs=[any_spec] * 4,
        out_specs=[any_spec] * 4,
        scratch_shapes=[
            pltpu.VMEM((4, block, width), BF16),
            dma((4, pieces)),
            dma((4, pieces)),
        ],
        compiler_params=pltpu.CompilerParams(vmem_limit_bytes=60 * 2**20),
    )(*parts)


def solution(mesh):
    in_specs = (P("seq", "head"), P(None, None, "head"), P("seq", "head", None), P("seq", "head"))
    out_specs = (P("seq", "head"), P("seq", "head"), P("seq", "head"), P("seq", "head"))
    return jax.shard_map(
        functools.partial(on_device, mesh.shape["seq"], mesh.shape["head"]),
        mesh=mesh,
        in_specs=in_specs,
        out_specs=out_specs,
        check_vma=False,
    )
```

```python
import functools

import jax
import jax.numpy as jnp
from jax import lax
from jax.experimental import pallas as pl
from jax.experimental.pallas import tpu as pltpu
from jax.sharding import PartitionSpec as P

MESH = pl.DeviceIdType.MESH
F32 = jnp.float32
BF16 = jnp.bfloat16


def dot_nn(a, b):
    return lax.dot_general(a, b, (((1,), (0,)), ((), ())), preferred_element_type=F32)


def dot_nt(a, b):
    return lax.dot_general(a, b, (((1,), (1,)), ((), ())), preferred_element_type=F32)


def dot_tn(a, b):
    return lax.dot_general(a, b, (((0,), (0,)), ((), ())), preferred_element_type=F32)


def level_factor(level):
    return 2.0 ** (-0.5 * (max(level, 1) - 1))


def diagonal_mask(rows, start, size, leaf, leaf_level):
    if size == leaf:
        total = jnp.zeros((leaf, leaf), F32)
        for level in range(leaf.bit_length()):
            row = rows[level : level + 1, start : start + leaf]
            total = jnp.where(leaf_level == level, row, total)
        return total
    half = size // 2
    early = diagonal_mask(rows, start, half, leaf, leaf_level)
    late = diagonal_mask(rows, start + half, half, leaf, leaf_level)
    level = half.bit_length()
    side = jnp.broadcast_to(
        rows[level : level + 1, start + half : start + size], (half, half)
    )
    return jnp.concatenate(
        [
            jnp.concatenate([early, side], 1),
            jnp.concatenate([jnp.zeros((half, half), F32), late], 1),
        ],
        0,
    )


def state_kernel(
    dims,
    act_ref,
    w_ref,
    lw_ref,
    cot_ref,
    out_ref,
    dq_ref,
    dk_ref,
    dv_ref,
    acts,
    w_vm,
    cot,
    partial,
    rows_vm,
    qkv,
    cots,
    qt_vm,
    kt_vm,
    vt_vm,
    ct_vm,
    group,
    rgrad,
    moving,
    s_send,
    s_recv,
    r_send,
    r_recv,
    upper,
    inner_t,
    inner,
    finals,
    act_sem,
    cot_sem,
    w_sem,
    act_send_sem,
    act_recv_sem,
    s_send_sem,
    s_recv_sem,
    r_send_sem,
    r_recv_sem,
    final_sem,
):
    n_seq, n_head, heads, head_dim, block, features, per = dims
    chunks = heads // per
    bits = n_seq.bit_length() - 1
    block_bits = block.bit_length() - 1
    scale = head_dim**-0.5
    width = per * head_dim
    seq = lax.axis_index("seq")
    head = lax.axis_index("head")
    bit_of = [lax.rem(seq // (1 << j), 2) for j in range(bits)]
    top = bits - 1
    below = bits - 2
    reach = 1 << below
    quarter = seq // reach
    partner_of = [seq + (1 << j) - 2 * (1 << j) * bit_of[j] for j in range(bits)]

    def weight_copy(c, chunk):
        return pltpu.make_async_copy(
            w_ref.at[c, :, pl.ds(pl.multiple_of(chunk * width, width), width)],
            w_vm.at[chunk, c],
            w_sem.at[c, chunk],
        )

    own_features = pl.ds(pl.multiple_of(head * features, features), features)
    own = pltpu.make_async_copy(act_ref, acts.at[:, own_features], act_sem)
    own.start()
    weight_copy(1, 0).start()
    weight_copy(2, 0).start()
    cot_copy = pltpu.make_async_copy(cot_ref, cot, cot_sem)

    barrier = pltpu.get_barrier_semaphore()
    for r in range(1, n_head):
        pl.semaphore_signal(
            barrier, inc=1, device_id=(seq, lax.rem(head + r, n_head)), device_id_type=MESH
        )
    for j in range(top):
        pl.semaphore_signal(barrier, inc=1, device_id=(partner_of[j], head), device_id_type=MESH)

    @pl.when((quarter == 1) | (quarter == 2))
    def _():
        other = seq + reach * (3 - 2 * quarter)
        pl.semaphore_signal(barrier, inc=1, device_id=(other, head), device_id_type=MESH)

    peers = n_head - 1 + top
    middle_half = (quarter == 1) | (quarter == 2)
    pl.when(middle_half)(lambda: pl.semaphore_wait(barrier, peers + 1))
    pl.when(jnp.logical_not(middle_half))(lambda: pl.semaphore_wait(barrier, peers))

    def act_copy(r):
        return pltpu.make_async_remote_copy(
            src_ref=act_ref,
            dst_ref=acts.at[:, own_features],
            send_sem=act_send_sem.at[r],
            recv_sem=act_recv_sem.at[r],
            device_id=(seq, lax.rem(head + r, n_head)),
            device_id_type=MESH,
        )

    for r in range(1, n_head):
        act_copy(r).start()

    levels = lw_ref.shape[0]
    for h in range(heads):
        rows_vm[h] = jnp.concatenate(
            [lw_ref[level, h : h + 1, :] * (scale * level_factor(level)) for level in range(levels)]
            + [jnp.zeros((1, block), F32)] * (-levels % 8),
            0,
        )
    stages = bits + 1

    def s_way(stage):
        if stage < below:
            return None, None, partner_of[stage]
        if stage == below:
            return bit_of[below] == 0, bit_of[below] == 1, partner_of[below]
        return quarter == stage - below, quarter == stage - below + 1, None

    def r_way(stage):
        if stage < 2:
            return quarter == 3 - stage, quarter == 2 - stage, None
        bit = bits - stage
        if stage == 2:
            return bit_of[below] == 1, bit_of[below] == 0, partner_of[below]
        return None, None, partner_of[bit]

    def remote(send, recv, send_sem, recv_sem, stage, chunk, target):
        return pltpu.make_async_remote_copy(
            src_ref=send.at[stage, chunk],
            dst_ref=recv.at[stage, chunk],
            send_sem=send_sem.at[stage, chunk],
            recv_sem=recv_sem.at[stage, chunk],
            device_id=(target, head),
            device_id_type=MESH,
        )

    def s_copy(stage, chunk):
        target = s_way(stage)[2]
        target = seq + reach if target is None else target
        return remote(s_send, s_recv, s_send_sem, s_recv_sem, stage, chunk, target)

    def r_copy(stage, chunk):
        target = r_way(stage)[2]
        target = seq - reach if target is None else target
        return remote(r_send, r_recv, r_send_sem, r_recv_sem, stage, chunk, target)

    def only_if(condition, action):
        if condition is None:
            action()
        else:
            pl.when(condition)(action)

    def start_s(stage, chunk):
        def send():
            s_send[stage, chunk] = group[chunk].astype(BF16)
            s_copy(stage, chunk).start()

        only_if(s_way(stage)[0], send)

    def start_r(stage, chunk):
        bit = top if stage < 2 else bits - stage

        def send():
            term = rgrad[chunk, :, bit]
            if stage == 1:
                term = term + moving[chunk]
            if stage >= 2:
                term = moving[chunk] + bit_of[bit].astype(F32) * term
            r_send[stage, chunk] = term.astype(BF16)
            r_copy(stage, chunk).start()

        only_if(r_way(stage)[0], send)

    zero = (per, head_dim, head_dim)

    def finish_s(stage, chunk):
        def take():
            s_copy(stage, chunk).wait_recv()
            got = s_recv[stage, chunk]
            if stage < below:
                flag = bit_of[stage].astype(F32)
                upper[chunk, :, stage] = (got.astype(F32) * flag).astype(BF16)
            else:
                upper[chunk, :, min(stage, top)] = got
            if stage <= below:
                group[chunk] += got.astype(F32)
            if stage == top:
                group[chunk] = got.astype(F32)

        if stage == below:

            @pl.when(bit_of[below] == 0)
            def _():
                upper[chunk, :, below] = jnp.zeros(zero, BF16)

        if stage == top:

            @pl.when(quarter < 2)
            def _():
                upper[chunk, :, top] = jnp.zeros(zero, BF16)

        only_if(s_way(stage)[1], take)

    def finish_r(stage, chunk):
        def take():
            r_copy(stage, chunk).wait_recv()
            got = r_recv[stage, chunk].astype(F32)
            if stage < 2:
                moving[chunk] = got
            else:
                moving[chunk] += got

        if stage == 0:
            moving[chunk] = jnp.zeros(zero, F32)
        if stage == 2:

            @pl.when(quarter == 2)
            def _():
                moving[chunk] = jnp.zeros(zero, F32)

        only_if(r_way(stage)[1], take)

    lag = 2
    heads_end = 2 * chunks + heads
    s_base, r_base = chunks, chunks + lag
    last_slot = r_base + lag * bits + chunks - 1
    crossing_inside = all(
        r_base + lag * bits + c >= 2 * chunks + per * (c + 1) - 1 for c in range(chunks)
    )

    def tick(slot, low, high):
        for stage in range(stages):
            for base, finish, start, is_r in (
                (s_base, finish_s, start_s, False),
                (r_base, finish_r, start_r, True),
            ):
                first = base + lag * stage
                if first > high or first + chunks - 1 < low:
                    continue
                chunk = slot - first

                @pl.when((chunk >= 0) & (chunk < chunks))
                def _():
                    finish(stage, chunk)
                    if stage < bits:
                        start(stage + 1, chunk)
                    elif is_r and crossing_inside:
                        cross(chunk)

    def final_copies(chunk):
        lanes = pl.ds(pl.multiple_of(chunk * width, width), width)
        return [
            pltpu.make_async_copy(
                finals.at[n, :, lanes], target.at[:, lanes], final_sem.at[n, chunk]
            )
            for n, target in enumerate((out_ref, dq_ref, dk_ref, dv_ref))
        ]

    def cross(chunk):
        for i in range(per):
            h = chunk * per + i
            lanes = pl.ds(pl.multiple_of(h * head_dim, head_dim), head_dim)
            weights = rows_vm[h]

            def weighted(transposed):
                full = transposed.astype(F32)
                parts = []
                for j in range(bits):
                    level = block_bits + 1 + j
                    parts.append((full * weights[level : level + 1, :]).astype(BF16))
                return jnp.concatenate(parts, 0)

            states = upper[chunk, i]
            tall = states.reshape(bits * head_dim, head_dim)
            wide = jnp.concatenate([states[j] for j in range(bits)], 1)
            out_t = inner_t[0, h] + dot_nn(tall.T, weighted(qt_vm[h]))
            dq_t = inner_t[1, h] + dot_nn(wide, weighted(ct_vm[h]))
            finals[0, :, lanes] = out_t.astype(BF16).T
            finals[1, :, lanes] = dq_t.astype(BF16).T
            suffix = moving[chunk, i].astype(BF16)
            finals[2, :, lanes] = (inner[0, h] + dot_nt(qkv[2, h], suffix)).astype(BF16)
            finals[3, :, lanes] = (inner[1, h] + dot_nn(qkv[1, h], suffix)).astype(BF16)
        for copy in final_copies(chunk):
            copy.start()

    own.wait()
    def keep(c, chunk, total):
        total = total.astype(BF16)
        for i in range(per):
            qkv[c, chunk * per + i] = total[:, i * head_dim : (i + 1) * head_dim]

    def project(c, chunk):
        keep(c, chunk, dot_nn(acts[...], w_vm[chunk, c]))

    def project_kv(chunk, _):
        for c in (1, 2):
            pl.when(chunk + 1 < chunks)(lambda: weight_copy(c, chunk + 1).start())
            weight_copy(c, chunk).wait()

        @pl.when(chunk == 0)
        def _():
            for c in (1, 2):
                partial[c - 1] = dot_nn(acts[:, own_features], w_vm[0, c, own_features, :])
            cot_copy.start()
            for r in range(1, n_head):
                act_copy(r).wait_recv()
            for c in (1, 2):
                total = partial[c - 1]
                for r in range(1, n_head):
                    other = lax.rem(head + n_head - r, n_head)
                    other = pl.ds(pl.multiple_of(other * features, features), features)
                    total += dot_nn(acts[:, other], w_vm[0, c, other, :])
                keep(c, 0, total)

        @pl.when(chunk > 0)
        def _():
            project(1, chunk)
            project(2, chunk)

        pl.when(chunk == chunks - 1)(lambda: weight_copy(0, 0).start())
        for i in range(per):
            h = chunk * per + i
            key_t = qkv[1, h].T
            group[chunk, i] = dot_nn(key_t, qkv[2, h])
            kt_vm[h] = key_t
            vt_vm[h] = qkv[2, h].T
        start_s(0, chunk)
        return 0

    lax.fori_loop(0, chunks, project_kv, 0)
    cot_copy.wait()

    def project_q(chunk, _):
        pl.when(chunk + 1 < chunks)(lambda: weight_copy(0, chunk + 1).start())
        weight_copy(0, chunk).wait()
        project(0, chunk)
        for i in range(per):
            h = chunk * per + i
            lanes = pl.ds(pl.multiple_of(h * head_dim, head_dim), head_dim)
            cotangent = cot[:, lanes]
            cots[h] = cotangent
            query_t = qkv[0, h].T
            wide = query_t.astype(F32)
            weights = rows_vm[h]
            for j in range(bits):
                level = block_bits + 1 + j
                weighted = (wide * weights[level : level + 1, :]).astype(BF16)
                rgrad[chunk, i, j] = dot_nn(weighted, cotangent)
            qt_vm[h] = query_t
            ct_vm[h] = cotangent.T
        start_r(0, chunk)
        tick(chunks + chunk, chunks, 2 * chunks - 1)
        return 0

    lax.fori_loop(0, chunks, project_q, 0)

    tile = min(2 * head_dim, block)
    leaf = min(head_dim, tile)
    tiles = block // tile
    early_ids = lax.broadcasted_iota(jnp.int32, (leaf, leaf), 0)
    late_ids = lax.broadcasted_iota(jnp.int32, (leaf, leaf), 1)
    differ = jnp.bitwise_xor(early_ids, late_ids)
    leaf_level = jnp.zeros((leaf, leaf), jnp.int32)
    for shift in range(leaf.bit_length() - 1):
        leaf_level = leaf_level + (differ >= (1 << shift)).astype(jnp.int32)
    leaf_level = jnp.where(early_ids <= late_ids, leaf_level, -1)

    def attend(h):
        weights = rows_vm[h]
        for a in range(tiles):
            here = slice(a * tile, (a + 1) * tile)
            end = (a + 1) * tile
            mask = []
            for b in range(a):
                level = tile.bit_length() - 1 + (a ^ b).bit_length()
                mask.append(jnp.broadcast_to(weights[level : level + 1, here], (tile, tile)))
            mask.append(diagonal_mask(weights, a * tile, tile, leaf, leaf_level))
            mask = jnp.concatenate(mask, 0) if a else mask[0]
            attn = (dot_nn(qkv[1, h, :end, :], qt_vm[h, :, here]) * mask).astype(BF16)
            grads = (dot_nn(qkv[2, h, :end, :], ct_vm[h, :, here]) * mask).astype(BF16)
            inner_t[0, h, :, here] = dot_nn(vt_vm[h, :, :end], attn)
            inner_t[1, h, :, here] = dot_nn(kt_vm[h, :, :end], grads)
            dk_part = dot_nn(grads, qkv[0, h, here, :])
            dv_part = dot_nn(attn, cots[h, here, :])
            if a:
                inner[0, h, : a * tile, :] += dk_part[: a * tile]
                inner[1, h, : a * tile, :] += dv_part[: a * tile]
            inner[0, h, here, :] = dk_part[a * tile :]
            inner[1, h, here, :] = dv_part[a * tile :]

    def middle(chunk, _):
        for i in range(per):
            attend(chunk * per + i)

        def advance(i, _):
            tick(2 * chunks + chunk * per + i, 2 * chunks, heads_end - 1)
            return 0

        lax.fori_loop(0, per, advance, 0)
        return 0

    lax.fori_loop(0, chunks, middle, 0)

    def settle(slot, _):
        tick(slot, heads_end, last_slot)
        return 0

    if last_slot >= heads_end:
        lax.fori_loop(heads_end, last_slot + 1, settle, 0)
    if not crossing_inside:

        def cross_one(chunk, _):
            cross(chunk)
            return 0

        lax.fori_loop(0, chunks, cross_one, 0)

    for r in range(1, n_head):
        act_copy(r).wait_send()

    def drain(chunk, _):
        for stage in range(stages):
            only_if(s_way(stage)[0], lambda: s_copy(stage, chunk).wait_send())
            only_if(r_way(stage)[0], lambda: r_copy(stage, chunk).wait_send())
        for copy in final_copies(chunk):
            copy.wait()
        return 0

    lax.fori_loop(0, chunks, drain, 0)


def hand_over_kernel(pieces, *refs):
    sources, targets, buffers = refs[:4], refs[4:8], refs[8]
    in_sem, out_sem = refs[9:]
    rows = sources[0].shape[0] // pieces
    order = [(n, piece) for piece in range(pieces) for n in range(4)]

    def copies(n, piece):
        part = pl.ds(piece * rows, rows)
        inward = pltpu.make_async_copy(
            sources[n].at[part], buffers.at[n, part], in_sem.at[n, piece]
        )
        outward = pltpu.make_async_copy(
            buffers.at[n, part], targets[n].at[part], out_sem.at[n, piece]
        )
        return inward, outward

    moves = [copies(n, piece) for n, piece in order]
    for inward, _ in moves:
        inward.start()
    for inward, outward in moves:
        inward.wait()
        outward.start()
    for _, outward in moves:
        outward.wait()


def on_device(n_seq, n_head, activations, w_proj, level_weight, grad_out):
    block, features = activations.shape
    width = w_proj.shape[2]
    heads = level_weight.shape[1]
    head_dim = width // heads
    per = 2 if heads % 2 == 0 else 1
    chunks = heads // per
    bits = n_seq.bit_length() - 1
    levels = level_weight.shape[2]
    padded = levels + (-levels % 8)
    dims = (n_seq, n_head, heads, head_dim, block, features, per)
    square = (head_dim, head_dim)
    tall = (block, head_dim)
    flat = (head_dim, block)
    dma = pltpu.SemaphoreType.DMA
    any_spec = pl.BlockSpec(memory_space=pl.ANY)
    vmem_spec = pl.BlockSpec(memory_space=pltpu.VMEM)
    results = [jax.ShapeDtypeStruct((block, width), BF16)] * 4
    parts = pl.pallas_call(
        functools.partial(state_kernel, dims),
        out_shape=results,
        in_specs=[any_spec, any_spec, vmem_spec, any_spec],
        out_specs=[any_spec] * 4,
        scratch_shapes=[
            pltpu.VMEM((block, n_head * features), BF16),
            pltpu.VMEM((chunks, 3, w_proj.shape[1], per * head_dim), BF16),
            pltpu.VMEM((block, width), BF16),
            pltpu.VMEM((2, block, per * head_dim), F32),
            pltpu.VMEM((heads, padded, block), F32),
            pltpu.VMEM((3, heads) + tall, BF16),
            pltpu.VMEM((heads,) + tall, BF16),
            pltpu.VMEM((heads,) + flat, BF16),
            pltpu.VMEM((heads,) + flat, BF16),
            pltpu.VMEM((heads,) + flat, BF16),
            pltpu.VMEM((heads,) + flat, BF16),
            pltpu.VMEM((chunks, per) + square, F32),
            pltpu.VMEM((chunks, per, bits) + square, F32),
            pltpu.VMEM((chunks, per) + square, F32),
            pltpu.VMEM((bits + 1, chunks, per) + square, BF16),
            pltpu.VMEM((bits + 1, chunks, per) + square, BF16),
            pltpu.VMEM((bits + 1, chunks, per) + square, BF16),
            pltpu.VMEM((bits + 1, chunks, per) + square, BF16),
            pltpu.VMEM((chunks, per, bits) + square, BF16),
            pltpu.VMEM((2, heads) + flat, F32),
            pltpu.VMEM((2, heads) + tall, F32),
            pltpu.VMEM((4, block, width), BF16),
            dma,
            dma,
            dma((3, chunks)),
            dma((n_head,)),
            dma((n_head,)),
            dma((bits + 1, chunks)),
            dma((bits + 1, chunks)),
            dma((bits + 1, chunks)),
            dma((bits + 1, chunks)),
            dma((4, chunks)),
        ],
        compiler_params=pltpu.CompilerParams(
            collective_id=0, has_side_effects=True, vmem_limit_bytes=56 * 2**20
        ),
    )(activations, w_proj, jnp.transpose(level_weight, (2, 1, 0)), grad_out)

    pieces = 2 if block % 256 == 0 else 1
    return pl.pallas_call(
        functools.partial(hand_over_kernel, pieces),
        out_shape=results,
        in_specs=[any_spec] * 4,
        out_specs=[any_spec] * 4,
        scratch_shapes=[
            pltpu.VMEM((4, block, width), BF16),
            dma((4, pieces)),
            dma((4, pieces)),
        ],
        compiler_params=pltpu.CompilerParams(vmem_limit_bytes=60 * 2**20),
    )(*parts)


def solution(mesh):
    in_specs = (P("seq", "head"), P(None, None, "head"), P("seq", "head", None), P("seq", "head"))
    out_specs = (P("seq", "head"), P("seq", "head"), P("seq", "head"), P("seq", "head"))
    return jax.shard_map(
        functools.partial(on_device, mesh.shape["seq"], mesh.shape["head"]),
        mesh=mesh,
        in_specs=in_specs,
        out_specs=out_specs,
        check_vma=False,
    )
```
